32 devices in a mesh: dp: 16 (over z, y, core), ctx: 2 (over x).
Axes of the slice: x: 2, y: 2, z: 4, core: 2. Of those that a mesh axis runs over, the one named last changes fastest.
Arguments:
- events: bfloat16 [8192, 512], P(('dp', 'ctx')), may hold values from -6 to 6
- out_grad: bfloat16 [8192, 512], P(('dp', 'ctx')), may hold values from -6 to 6
- proj_weight: bfloat16 [512, 2048], replicated, may hold values from -0.25 to 0.25
- out_weight: bfloat16 [512, 512], replicated, may hold values from -0.25 to 0.25
- lengths: int32 [16, 4], P('dp'), may hold values from 1 to 256, 512 in all within a row
- tile_mask: int32 [64, 4], P('dp'), may hold values 0 or 1
- quotient_shard: int32 [8192], P(('dp', 'ctx')), may hold values from 0 to 31, as said below
- quotient_row: int32 [8192], P(('dp', 'ctx')), may hold values from 0 to 65535
- remainder_shard: int32 [8192], P(('dp', 'ctx')), may hold values from 0 to 31, as said below
- remainder_row: int32 [8192], P(('dp', 'ctx')), may hold values from 0 to 65535
Outputs:
- quotient_grads: float32 [12288, 512], P(('dp', 'ctx'))
- remainder_grads: float32 [12288, 512], P(('dp', 'ctx'))
- proj_weight_grad: float32 [512, 2048], replicated
- out_weight_grad: float32 [512, 512], replicated
The draws below stay inside these ranges and needn't reach their ends.
Inputs may be any that keep to these rules, and one draw needn't show every extreme that they name: `quotient_shard`: in every device's 256 rows no shard is named more than 12 times, and some shard exactly 12 times. `remainder_shard`: in every device's 256 rows no shard is named more than 12 times, and some shard exactly 12 times.
All inputs are finite; a program needn't handle non-finite values. No bound on the sum of `tile_mask` on one device may be relied on, other than what follows from the above.
Results may differ from the reference program's by a relative error of at most 0.0068.
Values may be sent and summed in bfloat16 or wider, within the bound.
A program may use at most 128 MiB of HBM per device.

```python
import math
import jax
import jax.numpy as jnp
import numpy as np
from jax import lax

D = 512
HEADS = 8
TILE = 128
HIST = 4
ROWS_DEV = 65536
TOK_DEV = 256
HD = 64
LEN = 512
LMAX = 256
NT = 4
TOKENS = 8192
CAP = 12
SLOTS = 384
N_DP = 16
DEVICES = 32


def shard_owners(key, salt_value):
    base_key = jax.random.fold_in(key, salt_value)
    slot_count = DEVICES * CAP

    def one_block(block_index):
        block_key = jax.random.fold_in(base_key, block_index)
        key_scores, key_forced, key_order = jax.random.split(block_key, 3)
        scores = jax.random.permutation(key_scores, slot_count)
        forced = jax.random.randint(key_forced, (), 0, DEVICES)
        slot_ids = jnp.arange(slot_count)
        scores = jnp.where(slot_ids // CAP == forced, -1 - slot_ids % CAP, scores)
        chosen = jnp.argsort(scores, stable=True)[:TOK_DEV]
        chosen = chosen[jax.random.permutation(key_order, TOK_DEV)]
        return (chosen // CAP).astype(jnp.int32)
    return jax.lax.map(one_block, jnp.arange(TOKENS // TOK_DEV)).reshape(TOKENS)


def draw_quotient_shard(key, part):
    return shard_owners(key, 17)


def draw_remainder_shard(key, part):
    return shard_owners(key, 29)


def set_ends(array, rng, low, high):
    index_at = [jax.random.randint(jax.random.fold_in(rng, axis), (), 0, length) for axis, length in enumerate(array.shape)]
    longest = array.shape.index(max(array.shape))
    neighbour = index_at[:longest] + [(index_at[longest] + 1) % array.shape[longest]] + index_at[longest + 1:]
    return array.at[tuple(index_at)].set(low).at[tuple(neighbour)].set(high)


def strengthened(values, stream_key, source, target, shards_of, factor):
    def block_of(dim):
        return (jnp.arange(values.shape[dim]) // (values.shape[dim] // shards_of)).reshape((-1,) + (1,) * (values.ndim - 1 - dim))

    one_side = jax.random.permutation(stream_key, shards_of)[block_of(target)]
    far = (block_of(target) + shards_of // 2) % shards_of
    return jnp.where((block_of(source) == one_side) | (block_of(source) == far), factor * values, values)


def block_scale(rng, extent, cuts, smallest, largest):
    def one(dim, shards_of):
        heights = jax.random.uniform(jax.random.fold_in(jax.random.fold_in(rng, 6), dim), (shards_of,), jnp.float32, smallest / len(cuts), largest / len(cuts))
        return jnp.repeat(jnp.exp(heights), extent[dim] // shards_of).reshape((-1,) + (1,) * (len(extent) - dim - 1))

    loudness = one(*cuts[0])
    for cut in cuts[1:]:
        loudness = loudness * one(*cut)
    return loudness


def cumulative_ranks(amount, lean):
    weights = [(1 << 20) // math.isqrt(rank ** lean) + 1 for rank in range(1, amount + 1)]
    deviation = 1 + sum(weights) // (1 << 30)
    return np.cumsum(np.array([max(1, weight // deviation) for weight in weights]))


def ranked(key, dims, count, lean):
    grid = cumulative_ranks(count, lean)
    pick = jax.random.randint(jax.random.fold_in(key, 1), dims, 0, int(grid[count - 1]))
    grade = jnp.searchsorted(jnp.asarray(grid, jnp.int32), pick, side="right")
    return jax.random.permutation(jax.random.fold_in(key, 2), count)[grade].astype(jnp.int32)


def profile(number_of, total, limit, slope):
    portions = [(1 << 20) // math.isqrt(rank ** slope) + 1 for rank in range(2, number_of + 1)]
    rest, given = total - limit - (number_of - 1), [1] * (number_of - 1)
    while rest > 0:
        candidates = [i for i in range(number_of - 1) if given[i] < limit]
        mass, remaining = sum([portions[i] for i in candidates]), rest
        for i in candidates:
            more = min(limit - given[i], max(1, remaining * portions[i] // mass), rest)
            given[i] = given[i] + more
            rest = rest - more
    return np.array([limit] + given)


def ragged_sizes(stream_key, amount, total, most, slope):
    if amount == 2:
        one = jax.random.randint(stream_key, (), max(1, total - most), min(most, total - 1) + 1)
        return jnp.stack([one, total - one])
    sizes = jnp.asarray(profile(amount, total, most, slope), jnp.int32)
    couples = (amount - 1) // 2
    donor, receiver = sizes[1:1 + 2 * couples:2], sizes[2:2 + 2 * couples:2]
    room = jnp.minimum(donor - 1, most - receiver)
    shifted = jax.random.randint(jax.random.fold_in(stream_key, 1), (couples,), 0, 1 << 20) % (room + 1)
    sizes = sizes.at[1:1 + 2 * couples:2].set(donor - shifted).at[2:2 + 2 * couples:2].set(receiver + shifted)
    return sizes[jax.random.permutation(jax.random.fold_in(stream_key, 2), amount)]


def bell_draw(stream_key, shape, spread, bound, cuts=(), kind=jnp.bfloat16):
    array = jax.random.normal(stream_key, shape, jnp.float32) * spread
    if len(cuts) > 0:
        array = block_scale(stream_key, shape, cuts, -0.22, 0.18) * array
    return jnp.clip(array, min=-bound, max=bound).astype(kind)


def noise_with(rng, dims, deviation, limit, cuts, heavy, kind=jnp.bfloat16):
    result = deviation * jax.random.normal(rng, dims, jnp.float32)
    if cuts:
        result = result * block_scale(rng, dims, cuts, -0.22, 0.18)
    return jnp.clip(strengthened(result, jax.random.fold_in(rng, 3), *heavy), -limit, limit).astype(kind)


def setup_inputs(seed: int = 0) -> dict:
    seeds = jax.random.split(jax.random.key(seed), 11)
    events = noise_with(seeds[0], (TOKENS, D), 1.0, 6.0, ((0, 32),), (0, 1, 32, 2.75))
    out_grad = bell_draw(seeds[1], (TOKENS, D), 1.0, 6.0, ((0, 32),))
    proj_weight = bell_draw(seeds[2], (D, 4 * D), D ** -0.5, 0.25)
    out_weight = bell_draw(seeds[3], (D, D), D ** -0.5, 0.25)
    lengths = jax.vmap(lambda own: ragged_sizes(own, HIST, LEN, LMAX, 0))(jax.random.split(seeds[4], N_DP)).reshape((N_DP, HIST)).astype(jnp.int32)
    tile_mask = set_ends((jax.random.randint(seeds[5], (N_DP * NT, NT), 0, 4) < 3).astype(jnp.int32), jax.random.fold_in(seeds[5], 1), 0, 1)
    quotient_shard = draw_quotient_shard(jax.random.fold_in(seeds[10], 71), 0)
    quotient_row = set_ends(ranked(seeds[7], (TOKENS,), ROWS_DEV, 2), jax.random.fold_in(seeds[7], 3), 0, ROWS_DEV - 1).astype(jnp.int32)
    remainder_shard = draw_remainder_shard(jax.random.fold_in(seeds[10], 71), 0)
    remainder_row = set_ends(ranked(seeds[9], (TOKENS,), ROWS_DEV, 2), jax.random.fold_in(seeds[9], 3), 0, ROWS_DEV - 1).astype(jnp.int32)
    return {"events": events, "out_grad": out_grad, "proj_weight": proj_weight, "out_weight": out_weight, "lengths": lengths, "tile_mask": tile_mask, "quotient_shard": quotient_shard, "quotient_row": quotient_row, "remainder_shard": remainder_shard, "remainder_row": remainder_row}


EPSILON = 1e-05

def silu_grad(value, sigma):
    return sigma * (1.0 + value * (1.0 - sigma))

def group_backward(packed_group, proj_weight, out_weight):
    inputs, cotangent, history, tile_table = packed_group
    score_scale = 1.0 / math.sqrt(HD)
    projected = jnp.dot(inputs, proj_weight, preferred_element_type=jnp.float32)
    sigmoid_proj = jax.nn.sigmoid(projected)
    activated = (projected * sigmoid_proj).astype(jnp.bfloat16)
    gate_rows = activated[:, :D].astype(jnp.float32)
    value_heads = activated[:, D:2 * D].astype(jnp.float32).reshape(LEN, HEADS, HD)
    query_heads = activated[:, 2 * D:3 * D].astype(jnp.float32).reshape(LEN, HEADS, HD)
    key_heads = activated[:, 3 * D:].astype(jnp.float32).reshape(LEN, HEADS, HD)
    position = jnp.arange(LEN, dtype=jnp.int32)
    doc_ends = jnp.cumsum(history)
    doc_ids = lax.optimization_barrier(jnp.sum((position[:, None] >= doc_ends[None, :]).astype(jnp.int32), axis=1))
    tile_full = jnp.repeat(jnp.repeat(tile_table, TILE, axis=0), TILE, axis=1)
    visible = (doc_ids[:, None] == doc_ids[None, :]) & (position[None, :] <= position[:, None]) & (tile_full == 1)
    weight = visible.astype(jnp.float32) / LMAX
    scores = jnp.einsum('ihd,jhd->hij', query_heads, key_heads) * score_scale
    sigmoid_scores = jax.nn.sigmoid(scores)
    attention = (scores * sigmoid_scores * weight[None]).astype(jnp.bfloat16).astype(jnp.float32)
    mixed_rows = jnp.einsum('hij,jhd->ihd', attention, value_heads).reshape(LEN, D)
    row_mean = lax.optimization_barrier(jnp.mean(mixed_rows, axis=1, keepdims=True))
    centered = mixed_rows - row_mean
    inv_scale = lax.rsqrt(lax.optimization_barrier(jnp.mean(centered * centered, axis=1, keepdims=True)) + EPSILON)
    normed = centered * inv_scale
    gated_rows = (normed * gate_rows).astype(jnp.bfloat16)
    out_weight_grad = jnp.dot(gated_rows.T, cotangent, preferred_element_type=jnp.float32)
    grad_gated = jnp.dot(cotangent, out_weight.T, preferred_element_type=jnp.float32)
    grad_normed = grad_gated * gate_rows
    grad_gate = grad_gated * normed
    grad_mixed = (inv_scale * (grad_normed - lax.optimization_barrier(jnp.mean(grad_normed, axis=1, keepdims=True)) - normed * lax.optimization_barrier(jnp.mean(grad_normed * normed, axis=1, keepdims=True)))).astype(jnp.bfloat16)
    grad_heads = grad_mixed.astype(jnp.float32).reshape(LEN, HEADS, HD)
    grad_attention = jnp.einsum('ihd,jhd->hij', grad_heads, value_heads)
    grad_scores = (grad_attention * weight[None] * silu_grad(scores, sigmoid_scores)).astype(jnp.bfloat16).astype(jnp.float32)
    grad_values = jnp.einsum('hij,ihd->jhd', attention, grad_heads).reshape(LEN, D)
    grad_query = jnp.einsum('hij,jhd->ihd', grad_scores, key_heads).reshape(LEN, D) * score_scale
    grad_keys = jnp.einsum('hij,ihd->jhd', grad_scores, query_heads).reshape(LEN, D) * score_scale
    grad_projected = (jnp.concatenate([grad_gate, grad_values, grad_query, grad_keys], axis=1) * silu_grad(projected, sigmoid_proj)).astype(jnp.bfloat16)
    grad_events = cotangent.astype(jnp.float32) + jnp.dot(grad_projected, proj_weight.T, preferred_element_type=jnp.float32)
    proj_weight_grad = jnp.dot(inputs.T, grad_projected, preferred_element_type=jnp.float32)
    return (grad_events, proj_weight_grad, out_weight_grad)

def route_rows(grad_events, shards, table_rows):
    owners = shards.reshape(DEVICES, TOK_DEV)
    earlier = jnp.arange(TOK_DEV)[None, :] < jnp.arange(TOK_DEV)[:, None]

    def block_rank(owner_block):
        matches = (owner_block[:, None] == owner_block[None, :]) & earlier
        return lax.optimization_barrier(jnp.sum(matches.astype(jnp.int32), axis=1)).astype(jnp.int32)
    slot_rank = lax.map(block_rank, owners).reshape(TOKENS)
    sender = (jnp.arange(TOKENS) // TOK_DEV).astype(jnp.int32)
    target = shards * SLOTS + sender * CAP + slot_rank
    buffer = jnp.zeros((DEVICES * SLOTS, D), jnp.float32).at[target].set(grad_events)
    labels = jnp.full((DEVICES * SLOTS,), -1, jnp.int32).at[target].set(table_rows)

    def owner_total(packed_owner):
        owner_block, row_marks = packed_owner
        matches = ((row_marks[:, None] == row_marks[None, :]) & (row_marks[None, :] >= 0)).astype(jnp.float32)
        return jnp.dot(matches, owner_block, precision=lax.Precision.HIGHEST, preferred_element_type=jnp.float32)
    totals = lax.map(owner_total, (buffer.reshape(DEVICES, SLOTS, D), labels.reshape(DEVICES, SLOTS)))
    return totals.reshape(DEVICES * SLOTS, D)

def reference(events, out_grad, proj_weight, out_weight, lengths, tile_mask, quotient_shard, quotient_row, remainder_shard, remainder_row):
    packed_groups = (events.reshape(N_DP, LEN, D), out_grad.reshape(N_DP, LEN, D), lengths, tile_mask.reshape(N_DP, NT, NT))
    grad_events, proj_parts, out_parts = lax.map(lambda packed_group: group_backward(packed_group, proj_weight, out_weight), packed_groups)
    grad_events = grad_events.reshape(TOKENS, D)
    quotient_grads = route_rows(grad_events, quotient_shard, quotient_row)
    remainder_grads = route_rows(grad_events, remainder_shard, remainder_row)
    return (quotient_grads, remainder_grads, lax.optimization_barrier(jnp.sum(proj_parts, axis=0)), lax.optimization_barrier(jnp.sum(out_parts, axis=0)))
```

```python
import math

import jax
import jax.numpy as jnp
from jax import lax
from jax.experimental import pallas as pl
from jax.experimental.pallas import tpu as pltpu
from jax.sharding import PartitionSpec as P

HEADS = 8
TILE = 128


EPSILON = 1e-05


def passed_along(shard, axis, by):
    count = lax.axis_size(axis)
    pairs = [(i, i + by) for i in range(count) if 0 <= i + by < count]
    return lax.ppermute(shard, axis, pairs)


def from_behind(shard, axis, by):
    count = lax.axis_size(axis)
    return lax.ppermute(shard, axis, [(i, (i + by) % count) for i in range(count)])


def silu_grad(value, sigma):
    return sigma * (1.0 + value * (1.0 - sigma))


def visible_weight(history, tile_table, row_start, row_count, col_start, col_count, longest):
    row_pos = row_start + jnp.arange(row_count, dtype=jnp.int32)
    col_pos = col_start + jnp.arange(col_count, dtype=jnp.int32)
    doc_ends = jnp.cumsum(history)
    row_doc = jnp.sum((row_pos[:, None] >= doc_ends[None, :]).astype(jnp.int32), axis=1)
    col_doc = jnp.sum((col_pos[:, None] >= doc_ends[None, :]).astype(jnp.int32), axis=1)
    tile_ids = jnp.arange(tile_table.shape[0], dtype=jnp.int32)
    row_tiles = (row_pos[:, None] // TILE == tile_ids[None, :]).astype(jnp.float32)
    col_tiles = (col_pos[:, None] // TILE == tile_ids[None, :]).astype(jnp.float32)
    tile_rows = jnp.dot(row_tiles, tile_table.astype(jnp.float32), precision=lax.Precision.HIGHEST)
    tile_full = jnp.dot(tile_rows, col_tiles.T, precision=lax.Precision.HIGHEST)
    visible = (
        (row_doc[:, None] == col_doc[None, :])
        & (col_pos[None, :] <= row_pos[:, None])
        & (tile_full > 0.5)
    )
    return visible.astype(jnp.float32) / longest


def guarded(weight, compute, empty_result):
    return lax.cond(jnp.any(weight > 0.0), compute, lambda: empty_result)


def forward_block(query_heads, key_rows, value_rows, weight, score_scale):
    col_count = key_rows.shape[0]
    key_heads = key_rows.reshape(col_count, HEADS, -1)
    value_heads = value_rows.reshape(col_count, HEADS, -1)
    scores = (
        jnp.einsum("ihd,jhd->hij", query_heads, key_heads, preferred_element_type=jnp.float32)
        * score_scale
    )
    attention = (scores * jax.nn.sigmoid(scores) * weight[None]).astype(jnp.bfloat16)
    mixed_rows = jnp.einsum(
        "hij,jhd->ihd", attention, value_heads, preferred_element_type=jnp.float32
    )
    return mixed_rows.reshape(query_heads.shape[0], -1)


def backward_block(query_heads, grad_heads, key_rows, value_rows, weight, score_scale):
    col_count = key_rows.shape[0]
    row_count = query_heads.shape[0]
    key_heads = key_rows.reshape(col_count, HEADS, -1)
    value_heads = value_rows.reshape(col_count, HEADS, -1)
    scores = (
        jnp.einsum("ihd,jhd->hij", query_heads, key_heads, preferred_element_type=jnp.float32)
        * score_scale
    )
    sigmoid_scores = jax.nn.sigmoid(scores)
    attention = (scores * sigmoid_scores * weight[None]).astype(jnp.bfloat16)
    grad_attention = jnp.einsum(
        "ihd,jhd->hij", grad_heads, value_heads, preferred_element_type=jnp.float32
    )
    grad_scores = (grad_attention * weight[None] * silu_grad(scores, sigmoid_scores)).astype(
        jnp.bfloat16
    )
    grad_values = jnp.einsum(
        "hij,ihd->jhd", attention, grad_heads, preferred_element_type=jnp.float32
    ).reshape(col_count, -1)
    grad_query = (
        jnp.einsum(
            "hij,jhd->ihd", grad_scores, key_heads, preferred_element_type=jnp.float32
        ).reshape(row_count, -1)
        * score_scale
    )
    grad_keys = (
        jnp.einsum(
            "hij,ihd->jhd", grad_scores, query_heads, preferred_element_type=jnp.float32
        ).reshape(col_count, -1)
        * score_scale
    )
    return (grad_query, grad_keys, grad_values)


def pack_rows(grad_events, shards, table_rows, data_size, loop_size, capacity):
    row_count, model_width = grad_events.shape
    slot_count = data_size * loop_size * capacity
    earlier = jnp.arange(row_count)[None, :] < jnp.arange(row_count)[:, None]
    matches = (shards[:, None] == shards[None, :]) & earlier
    slot_rank = jnp.sum(matches.astype(jnp.int32), axis=1)
    target = shards * capacity + slot_rank
    onehot = jnp.arange(slot_count, dtype=jnp.int32)[:, None] == target[None, :]
    packed = jnp.dot(
        onehot.astype(jnp.float32),
        grad_events,
        precision=lax.Precision.HIGHEST,
        preferred_element_type=jnp.float32,
    )
    labels = jnp.sum(jnp.where(onehot, table_rows[None, :] + 1, 0), axis=1) - 1
    return (
        packed.reshape(data_size, loop_size, capacity, model_width),
        labels.reshape(data_size, loop_size, capacity),
    )


def merge_rows(received, row_marks):
    model_width = received.shape[-1]
    flat_rows = received.reshape(-1, model_width)
    flat_marks = row_marks.reshape(-1)
    matches = ((flat_marks[:, None] == flat_marks[None, :]) & (flat_marks[None, :] >= 0)).astype(
        jnp.float32
    )
    return jnp.dot(
        matches, flat_rows, precision=lax.Precision.HIGHEST, preferred_element_type=jnp.float32
    )


def body(
    events,
    out_grad,
    proj_weight,
    out_weight,
    lengths,
    tile_mask,
    quotient_shard,
    quotient_row,
    remainder_shard,
    remainder_row,
):
    row_count, model_width = events.shape
    loop_size = lax.axis_size("ctx")
    data_size = lax.axis_size("dp")
    loop_place = lax.axis_index("ctx")
    longest = float(row_count * loop_size // 2)
    score_scale = 1.0 / math.sqrt(model_width // HEADS)
    history = lengths[0]
    row_start = loop_place * row_count
    projected = jnp.dot(events, proj_weight, preferred_element_type=jnp.float32)
    sigmoid_proj = jax.nn.sigmoid(projected)
    activated = (projected * sigmoid_proj).astype(jnp.bfloat16)
    gate_rows = activated[:, :model_width].astype(jnp.float32)
    value_rows = activated[:, model_width : 2 * model_width]
    query_rows = activated[:, 2 * model_width : 3 * model_width]
    key_rows = activated[:, 3 * model_width :]
    query_heads = query_rows.reshape(row_count, HEADS, -1)
    empty_rows = jnp.zeros((row_count, model_width), jnp.float32)

    def forward_turn(turn_index, state):
        running, key_block, value_block = state
        offset_row = (loop_place - turn_index) % loop_size * row_count
        weight = visible_weight(
            history, tile_mask, row_start, row_count, offset_row, row_count, longest
        )
        running = running + guarded(
            weight,
            lambda: forward_block(query_heads, key_block, value_block, weight, score_scale),
            empty_rows,
        )
        key_next, value_next = passed_along((key_block, value_block), "ctx", 1)
        return (running, key_next, value_next)

    mixed_rows, key_spent, value_spent = lax.fori_loop(
        0, loop_size, forward_turn, (empty_rows, key_rows, value_rows)
    )
    row_mean = jnp.mean(mixed_rows, axis=1, keepdims=True)
    centered = mixed_rows - row_mean
    inv_scale = lax.rsqrt(jnp.mean(centered * centered, axis=1, keepdims=True) + EPSILON)
    normed = centered * inv_scale
    gated_rows = (normed * gate_rows).astype(jnp.bfloat16)
    out_weight_term = jnp.einsum(
        "td,te->de", gated_rows, out_grad, preferred_element_type=jnp.float32
    )
    grad_gated = jnp.einsum("te,de->td", out_grad, out_weight, preferred_element_type=jnp.float32)
    grad_normed = grad_gated * gate_rows
    grad_gate = grad_gated * normed
    grad_mixed = (
        inv_scale
        * (
            grad_normed
            - jnp.mean(grad_normed, axis=1, keepdims=True)
            - normed * jnp.mean(grad_normed * normed, axis=1, keepdims=True)
        )
    ).astype(jnp.bfloat16)
    grad_heads = grad_mixed.reshape(row_count, HEADS, -1)
    empty_triple = (empty_rows, empty_rows, empty_rows)

    def cycle_turn(turn_index, state):
        grad_query, key_block, value_block, key_grad_block, value_grad_block = state
        offset_row = (loop_place - turn_index) % loop_size * row_count
        weight = visible_weight(
            history, tile_mask, row_start, row_count, offset_row, row_count, longest
        )
        query_add, key_add, value_add = guarded(
            weight,
            lambda: backward_block(
                query_heads, grad_heads, key_block, value_block, weight, score_scale
            ),
            empty_triple,
        )
        key_next, value_next = passed_along((key_block, value_block), "ctx", 1)
        key_grad_next, value_grad_next = from_behind(
            (key_grad_block + key_add, value_grad_block + value_add), "ctx", 1
        )
        return (grad_query + query_add, key_next, value_next, key_grad_next, value_grad_next)

    grad_query, key_back, value_back, grad_keys, grad_values = lax.fori_loop(
        0, loop_size, cycle_turn, (empty_rows, key_rows, value_rows, empty_rows, empty_rows)
    )
    grad_projected = (
        jnp.concatenate([grad_gate, grad_values, grad_query, grad_keys], axis=1)
        * silu_grad(projected, sigmoid_proj)
    ).astype(jnp.bfloat16)
    grad_events = out_grad.astype(jnp.float32) + jnp.einsum(
        "tf,df->td", grad_projected, proj_weight, preferred_element_type=jnp.float32
    )
    proj_weight_term = jnp.einsum(
        "td,tf->df", events, grad_projected, preferred_element_type=jnp.float32
    )
    proj_weight_grad, out_weight_grad = lax.psum((proj_weight_term, out_weight_term), ("dp", "ctx"))
    devices = data_size * loop_size
    capacity = max(2, 3 * row_count // (2 * devices))
    quotient_buffer, quotient_labels = pack_rows(
        grad_events, quotient_shard, quotient_row, data_size, loop_size, capacity
    )
    remainder_buffer, remainder_labels = pack_rows(
        grad_events, remainder_shard, remainder_row, data_size, loop_size, capacity
    )
    quotient_in, remainder_in, quotient_marks, remainder_marks = (
        lax.all_to_all(
            lax.all_to_all(quotient_buffer, "dp", split_axis=0, concat_axis=0, tiled=True),
            "ctx",
            split_axis=1,
            concat_axis=1,
            tiled=True,
        ),
        lax.all_to_all(
            lax.all_to_all(remainder_buffer, "dp", split_axis=0, concat_axis=0, tiled=True),
            "ctx",
            split_axis=1,
            concat_axis=1,
            tiled=True,
        ),
        lax.all_to_all(
            lax.all_to_all(quotient_labels, "dp", split_axis=0, concat_axis=0, tiled=True),
            "ctx",
            split_axis=1,
            concat_axis=1,
            tiled=True,
        ),
        lax.all_to_all(
            lax.all_to_all(remainder_labels, "dp", split_axis=0, concat_axis=0, tiled=True),
            "ctx",
            split_axis=1,
            concat_axis=1,
            tiled=True,
        ),
    )
    quotient_grads = merge_rows(quotient_in, quotient_marks)
    remainder_grads = merge_rows(remainder_in, remainder_marks)
    return (quotient_grads, remainder_grads, proj_weight_grad, out_weight_grad)


F32 = jnp.float32
BF16 = jnp.bfloat16
MESH = pl.DeviceIdType.MESH
BLOCK = 32
WIDTH = 512


def dot_rows(a, b):
    return lax.dot_general(a, b, (((1,), (1,)), ((), ())), preferred_element_type=F32)


def dot_first(a, b):
    return lax.dot_general(a, b, (((0,), (0,)), ((), ())), preferred_element_type=F32)


def sigmoid_of(x):
    return 0.5 * jnp.tanh(0.5 * x) + 0.5


def layer_kernel(
    place_ref, lengths_ref, tiles_ref, ev_own, og_own, ev_far, og_far, weight_ref, out_weight_ref,
    shards_ref, rows_ref, pack_ref, wgrad_ref,
    ev, og, act, dact, att, slope, mixed, gm, mask, gp, gated,
):
    half, width = ev_own.shape
    full = 2 * half
    place = place_ref[0]
    own = pl.multiple_of(place * half, half)
    far = pl.multiple_of((1 - place) * half, half)
    ev[pl.ds(own, half), :] = ev_own[...]
    ev[pl.ds(far, half), :] = ev_far[...]
    og[pl.ds(own, half), :] = og_own[...]
    og[pl.ds(far, half), :] = og_far[...]

    ends = []
    total = jnp.int32(0)
    for k in range(lengths_ref.shape[1]):
        total = total + lengths_ref[0, k]
        ends.append(total)
    longest = float(full // 2)
    tiles = full // TILE
    mask[...] = jnp.zeros_like(mask)
    for a in range(tiles):
        row = a * TILE + lax.broadcasted_iota(jnp.int32, (TILE, TILE), 0)
        row_doc = sum((row >= e).astype(jnp.int32) for e in ends)
        for b in range(a + 1):
            col = b * TILE + lax.broadcasted_iota(jnp.int32, (TILE, TILE), 1)
            col_doc = sum((col >= e).astype(jnp.int32) for e in ends)
            keep = jnp.where(tiles_ref[a, b] == 1, 1.0 / longest, 0.0)
            seen = (row_doc == col_doc) & (col <= row)
            mask[a * TILE : (a + 1) * TILE, b * TILE : (b + 1) * TILE] = jnp.where(seen, keep, 0.0)

    @pl.loop(0, 4 * width // 256)
    def _(n):
        cols = pl.ds(pl.multiple_of(n * 256, 256), 256)
        projected = jnp.dot(ev[...], weight_ref[:, cols], preferred_element_type=F32)
        sig = sigmoid_of(projected)
        value = projected * sig
        act[:, cols] = value.astype(BF16)
        dact[:, cols] = sig * (1.0 + projected * (1.0 - sig))

    scale = 1.0 / math.sqrt(width // HEADS)
    head_width = width // HEADS
    lane = lax.broadcasted_iota(jnp.int32, (1, 128), 1) // head_width

    def pair_cols(base, p):
        return pl.ds(pl.multiple_of(base * width + p * 128, 128), 128)

    def only(x, h):
        return jnp.where(lane == h, x, jnp.zeros_like(x))

    blocks = ((0, half), (half, full))

    @pl.loop(0, width // 128)
    def _(p):
        q = (act[:, pair_cols(2, p)].astype(F32) * scale).astype(BF16)
        k = act[:, pair_cols(3, p)]
        v = act[:, pair_cols(1, p)]
        for lo, hi in blocks:
            total = jnp.zeros((half, 128), F32)
            for h in range(2):
                scores = dot_rows(only(q[lo:hi], h), k[:hi])
                sig = sigmoid_of(scores)
                w = mask[lo:hi, :hi]
                a = (scores * sig * w).astype(BF16)
                att[p * 2 + h, lo:hi, :hi] = a
                slope[p * 2 + h, lo:hi, :hi] = w * sig * (1.0 + scores * (1.0 - sig))
                total = total + jnp.dot(a, only(v[:hi], h), preferred_element_type=F32)
            mixed[lo:hi, pl.ds(pl.multiple_of(p * 128, 128), 128)] = total

    @pl.loop(0, full // 128)
    def _(r):
        rows = pl.ds(pl.multiple_of(r * 128, 128), 128)
        m = mixed[rows, :]
        centered = m - jnp.mean(m, axis=1, keepdims=True)
        inv = lax.rsqrt(jnp.mean(centered * centered, axis=1, keepdims=True) + EPSILON)
        normed = centered * inv
        gate = act[rows, :width].astype(F32)
        gated[rows, :] = (normed * gate).astype(BF16)
        grad_gated = dot_rows(og[rows, :], out_weight_ref[...])
        grad_normed = grad_gated * gate
        gp[rows, :width] = (grad_gated * normed * dact[rows, :width]).astype(BF16)
        gm[rows, :] = (
            inv
            * (
                grad_normed
                - jnp.mean(grad_normed, axis=1, keepdims=True)
                - normed * jnp.mean(grad_normed * normed, axis=1, keepdims=True)
            )
        ).astype(BF16)

    @pl.loop(0, width // 128)
    def _(p):
        q = (act[:, pair_cols(2, p)].astype(F32) * scale).astype(BF16)
        k = act[:, pair_cols(3, p)]
        v = act[:, pair_cols(1, p)]
        g = gm[:, pair_cols(0, p)]
        dv = [jnp.zeros((half, 128), F32)] * 2
        dk = [jnp.zeros((half, 128), F32)] * 2
        dq = [jnp.zeros((half, 128), F32)] * 2
        for h in range(2):
            kh, gh, qh = only(k, h), only(g, h), only(q, h)
            for n, (lo, hi) in enumerate(blocks):
                grad_att = dot_rows(gh[lo:hi], v[:hi])
                gs = (grad_att * slope[p * 2 + h, lo:hi, :hi]).astype(BF16)
                dq[n] = dq[n] + jnp.dot(gs, kh[:hi], preferred_element_type=F32)
                a = att[p * 2 + h, lo:hi, :hi]
                for m in range(n + 1):
                    at = slice(m * half, (m + 1) * half)
                    dv[m] = dv[m] + dot_first(a[:, at], gh[lo:hi])
                    dk[m] = dk[m] + dot_first(gs[:, at], qh[lo:hi])
        for n, (lo, hi) in enumerate(blocks):
            for base, value in ((1, dv[n]), (2, dq[n] * scale), (3, dk[n])):
                cols = pair_cols(base, p)
                gp[lo:hi, cols] = (value * dact[lo:hi, cols]).astype(BF16)

    mine = pl.ds(own, half)
    wgrad_ref[:, 4 * width :] = dot_first(gated[:, mine], og[...]).astype(BF16)
    ev_mine = ev[:, mine]

    @pl.loop(0, 4 * width // 512)
    def _(n):
        cols = pl.ds(pl.multiple_of(n * 512, 512), 512)
        wgrad_ref[:, cols] = dot_first(ev_mine, gp[:, cols]).astype(BF16)

    grad_events = (og_own[...].astype(F32) + dot_rows(gp[mine, :], weight_ref[...])).astype(BF16)

    slots = pack_ref.shape[0]
    capacity = 3 * half // (2 * (slots // BLOCK))
    early = lax.broadcasted_iota(jnp.int32, (half, half), 0) < lax.broadcasted_iota(
        jnp.int32, (half, half), 1
    )
    slot = lax.broadcasted_iota(jnp.int32, (slots, half), 0)
    spot = lax.broadcasted_iota(jnp.int32, (128, half), 0)
    onehot = jnp.zeros((slots, half), F32)
    numbers = jnp.zeros((slots, 128), F32)
    for t in range(2):
        shard = shards_ref[t : t + 1, :]
        across = jnp.broadcast_to(shard.astype(F32), (half, half))
        same = (jnp.transpose(across) == across) & early
        rank = jnp.sum(same.astype(F32), axis=0, keepdims=True).astype(jnp.int32)
        at = rank + t * capacity
        onehot = onehot + (slot == shard * BLOCK + at).astype(F32)
        number = rows_ref[t : t + 1, :]
        high = (number // 256 + 1).astype(F32)
        low = (number % 256).astype(F32)
        left = jnp.where(slot == shard * BLOCK + 2 * capacity, high, 0.0) + jnp.where(
            slot == shard * BLOCK + 2 * capacity + 1, low, 0.0
        )
        numbers = numbers + dot_rows(left.astype(BF16), (spot == at).astype(BF16))
    onehot = onehot.astype(BF16)
    packed = jnp.dot(onehot, grad_events, preferred_element_type=F32)
    pack_ref[:, :128] = (packed[:, :128] + numbers).astype(BF16)
    pack_ref[:, 128:] = packed[:, 128:].astype(BF16)


def exchange_kernel(
    data_size, pack_ref, wgrad_ref, got_ref, sum_ref,
    totals, outgo, income, local_sem, row_send, row_recv, red_send, red_recv, all_send, all_recv,
):
    data = lax.axis_index("dp")
    place = lax.axis_index("ctx")
    me = data * 2 + place
    devices = data_size * 2
    barrier = pltpu.get_barrier_semaphore()

    def other(k):
        to = lax.rem(me + k, devices)
        return to, (to // 2, lax.rem(to, 2))

    @pl.loop(1, devices)
    def _(k):
        _, where = other(k)
        pl.semaphore_signal(barrier, inc=1, device_id=where, device_id_type=MESH)

    pl.semaphore_wait(barrier, devices - 1)

    steps = data_size.bit_length() - 1
    height = wgrad_ref.shape[0]

    def bit(n):
        return lax.rem(data // (1 << n), 2)

    def toward(n):
        return (data + (1 - 2 * bit(n)) * (1 << n), place)

    def remote(src, dst, send, recv, where):
        return pltpu.make_async_remote_copy(
            src_ref=src, dst_ref=dst, send_sem=send, recv_sem=recv, device_id=where,
            device_id_type=MESH,
        )

    def reduce_copy(n):
        size = height >> (n + 1)
        if n == 0:
            src = wgrad_ref.at[pl.ds(pl.multiple_of((1 - bit(0)) * size, size), size)]
        else:
            src = outgo.at[pl.ds(height - 2 * size, size)]
        dst = income.at[pl.ds(height - 2 * size, size)]
        return remote(src, dst, red_send.at[n], red_recv.at[n], toward(n))

    first = reduce_copy(0)
    first.start()

    def row_copy(k):
        to, where = other(k)
        return remote(
            pack_ref.at[pl.ds(pl.multiple_of(to * BLOCK, BLOCK), BLOCK)],
            got_ref.at[pl.ds(pl.multiple_of(me * BLOCK, BLOCK), BLOCK)],
            row_send.at[k],
            row_recv.at[k],
            where,
        )

    here = pl.ds(pl.multiple_of(me * BLOCK, BLOCK), BLOCK)
    local = pltpu.make_async_copy(pack_ref.at[here], got_ref.at[here], local_sem)
    local.start()

    @pl.loop(1, devices)
    def _(k):
        row_copy(k).start()

    offset = place * height
    for n in range(steps):
        size = height >> (n + 1)
        came = pl.ds(height - 2 * size, size)
        reduce_copy(n).wait_recv()
        kept = pl.ds(pl.multiple_of(bit(n) * size, size), size)
        if n == 0:
            held = wgrad_ref[kept, :].astype(F32)
        else:
            held = totals[kept, :]
        held = held + income[came, :].astype(F32)
        offset = offset + bit(n) * size
        if n + 1 < steps:
            totals[:size, :] = held
            part = size // 2
            gone = pl.ds(pl.multiple_of((1 - bit(n + 1)) * part, part), part)
            outgo[pl.ds(height - 2 * part, part), :] = totals[gone, :].astype(BF16)
            reduce_copy(n + 1).start()
        else:
            sum_ref[pl.ds(pl.multiple_of(offset, size), size), :] = held.astype(BF16)

    def spread(n, start, size, where):
        rows = sum_ref.at[pl.ds(pl.multiple_of(start, size), size)]
        return remote(rows, rows, all_send.at[n], all_recv.at[n], where)

    size = height >> steps
    sent = []
    for n in range(steps - 1, 0, -1):
        copy = spread(n, offset, size, toward(n))
        copy.start()
        sent.append(copy)
        copy.wait_recv()
        offset = offset - bit(n) * size
        size = 2 * size
    ctx_copy = spread(steps, offset, size, (data, 1 - place))
    ctx_copy.start()
    near = spread(0, offset, size, toward(0))
    near.start()
    ctx_copy.wait_recv()
    back = spread(steps + 1, offset + (1 - 2 * place) * height, size, toward(0))
    back.start()
    near.wait_recv()
    back.wait_recv()
    for copy in sent + [ctx_copy, near, back]:
        copy.wait_send()
    for n in range(steps):
        reduce_copy(n).wait_send()
    local.wait()

    @pl.loop(1, devices)
    def _(k):
        copy = row_copy(k)
        copy.wait_send()
        copy.wait_recv()


def pair_body(
    events, out_grad, proj_weight, out_weight, lengths, tile_mask,
    quotient_shard, quotient_row, remainder_shard, remainder_row,
):
    half, width = events.shape
    data_size = lax.axis_size("dp")
    devices = 2 * data_size
    capacity = 3 * half // (2 * devices)
    full = 2 * half
    swap = [(0, 1), (1, 0)]
    ev_far = lax.ppermute(events, "ctx", swap)
    og_far = lax.ppermute(out_grad, "ctx", swap)
    place = lax.axis_index("ctx").astype(jnp.int32).reshape(1)
    shards = jnp.stack([quotient_shard, remainder_shard])
    numbers = jnp.stack([quotient_row, remainder_row])
    vmem = pl.BlockSpec(memory_space=pltpu.VMEM)
    smem = pl.BlockSpec(memory_space=pltpu.SMEM)
    packed, wgrad = pl.pallas_call(
        layer_kernel,
        name="layer",
        out_shape=(
            jax.ShapeDtypeStruct((devices * BLOCK, width), BF16),
            jax.ShapeDtypeStruct((half, 5 * width), BF16),
        ),
        in_specs=[smem] * 3 + [vmem] * 8,
        out_specs=(vmem, vmem),
        scratch_shapes=[
            pltpu.VMEM((full, width), BF16),
            pltpu.VMEM((full, width), BF16),
            pltpu.VMEM((full, 4 * width), BF16),
            pltpu.VMEM((full, 4 * width), F32),
            pltpu.VMEM((HEADS, full, full), BF16),
            pltpu.VMEM((HEADS, full, full), F32),
            pltpu.VMEM((full, width), F32),
            pltpu.VMEM((full, width), BF16),
            pltpu.VMEM((full, full), F32),
            pltpu.VMEM((full, 4 * width), BF16),
            pltpu.VMEM((full, width), BF16),
        ],
        compiler_params=pltpu.CompilerParams(vmem_limit_bytes=56 * 2**20),
        cost_estimate=pl.CostEstimate(
            flops=10 * 10**9, bytes_accessed=8 * 2**20, transcendentals=4 * 10**6
        ),
    )(
        place, lengths, tile_mask, events, out_grad, ev_far, og_far, proj_weight, out_weight,
        shards, numbers,
    )
    steps = data_size.bit_length() - 1
    got, sums = pl.pallas_call(
        lambda *refs: exchange_kernel(data_size, *refs),
        name="exchange",
        out_shape=(
            jax.ShapeDtypeStruct((devices * BLOCK, width), BF16),
            jax.ShapeDtypeStruct((full, 5 * width), BF16),
        ),
        in_specs=[vmem, vmem],
        out_specs=(vmem, vmem),
        scratch_shapes=[
            pltpu.VMEM((half // 2, 5 * width), F32),
            pltpu.VMEM((half, 5 * width), BF16),
            pltpu.VMEM((half, 5 * width), BF16),
            pltpu.SemaphoreType.DMA,
            pltpu.SemaphoreType.DMA((devices,)),
            pltpu.SemaphoreType.DMA((devices,)),
            pltpu.SemaphoreType.DMA((steps,)),
            pltpu.SemaphoreType.DMA((steps,)),
            pltpu.SemaphoreType.DMA((steps + 2,)),
            pltpu.SemaphoreType.DMA((steps + 2,)),
        ],
        compiler_params=pltpu.CompilerParams(
            collective_id=0, has_side_effects=True, vmem_limit_bytes=40 * 2**20
        ),
        cost_estimate=pl.CostEstimate(flops=10**6, bytes_accessed=8 * 2**20, transcendentals=0),
    )(packed, wgrad)
    blocks = got.reshape(devices, BLOCK, width)
    head = blocks[:, 2 * capacity : 2 * capacity + 2, : 2 * capacity].astype(jnp.int32)
    marks = jnp.where(head[:, 0] > 0, (head[:, 0] - 1) * 256 + head[:, 1], -1)
    blank = jnp.full((devices, BLOCK), -1, jnp.int32)
    grads = []
    for t in range(2):
        mine = marks[:, t * capacity : (t + 1) * capacity]
        keys = lax.dynamic_update_slice(blank, mine, (0, t * capacity)).reshape(-1)
        slots = mine.reshape(-1)
        matches = (slots[:, None] == keys[None, :]) & (keys[None, :] >= 0)
        grads.append(jnp.dot(matches.astype(BF16), got, preferred_element_type=F32))
    return (
        grads[0],
        grads[1],
        sums[:, : 4 * width].astype(F32),
        sums[:, 4 * width :].astype(F32),
    )


def pair_fits(mesh):
    data_size, loop_size = mesh.shape["dp"], mesh.shape["ctx"]
    return loop_size == 2 and data_size == 16


def solution(mesh):
    chosen = pair_body if pair_fits(mesh) else body
    in_specs = (
        P(("dp", "ctx"), None),
        P(("dp", "ctx"), None),
        P(),
        P(),
        P("dp", None),
        P("dp", None),
        P(("dp", "ctx")),
        P(("dp", "ctx")),
        P(("dp", "ctx")),
        P(("dp", "ctx")),
    )
    out_specs = (P(("dp", "ctx"), None), P(("dp", "ctx"), None), P(), P())
    return jax.shard_map(chosen, mesh=mesh, in_specs=in_specs, out_specs=out_specs, check_vma=False)
```

```python
import math

import jax
import jax.numpy as jnp
from jax import lax
from jax.experimental import pallas as pl
from jax.experimental.pallas import tpu as pltpu
from jax.sharding import PartitionSpec as P

HEADS = 8
TILE = 128


EPSILON = 1e-05


def passed_along(shard, axis, by):
    count = lax.axis_size(axis)
    pairs = [(i, i + by) for i in range(count) if 0 <= i + by < count]
    return lax.ppermute(shard, axis, pairs)


def from_behind(shard, axis, by):
    count = lax.axis_size(axis)
    return lax.ppermute(shard, axis, [(i, (i + by) % count) for i in range(count)])


def silu_grad(value, sigma):
    return sigma * (1.0 + value * (1.0 - sigma))


def visible_weight(history, tile_table, row_start, row_count, col_start, col_count, longest):
    row_pos = row_start + jnp.arange(row_count, dtype=jnp.int32)
    col_pos = col_start + jnp.arange(col_count, dtype=jnp.int32)
    doc_ends = jnp.cumsum(history)
    row_doc = jnp.sum((row_pos[:, None] >= doc_ends[None, :]).astype(jnp.int32), axis=1)
    col_doc = jnp.sum((col_pos[:, None] >= doc_ends[None, :]).astype(jnp.int32), axis=1)
    tile_ids = jnp.arange(tile_table.shape[0], dtype=jnp.int32)
    row_tiles = (row_pos[:, None] // TILE == tile_ids[None, :]).astype(jnp.float32)
    col_tiles = (col_pos[:, None] // TILE == tile_ids[None, :]).astype(jnp.float32)
    tile_rows = jnp.dot(row_tiles, tile_table.astype(jnp.float32), precision=lax.Precision.HIGHEST)
    tile_full = jnp.dot(tile_rows, col_tiles.T, precision=lax.Precision.HIGHEST)
    visible = (
        (row_doc[:, None] == col_doc[None, :])
        & (col_pos[None, :] <= row_pos[:, None])
        & (tile_full > 0.5)
    )
    return visible.astype(jnp.float32) / longest


def guarded(weight, compute, empty_result):
    return lax.cond(jnp.any(weight > 0.0), compute, lambda: empty_result)


def forward_block(query_heads, key_rows, value_rows, weight, score_scale):
    col_count = key_rows.shape[0]
    key_heads = key_rows.reshape(col_count, HEADS, -1)
    value_heads = value_rows.reshape(col_count, HEADS, -1)
    scores = (
        jnp.einsum("ihd,jhd->hij", query_heads, key_heads, preferred_element_type=jnp.float32)
        * score_scale
    )
    attention = (scores * jax.nn.sigmoid(scores) * weight[None]).astype(jnp.bfloat16)
    mixed_rows = jnp.einsum(
        "hij,jhd->ihd", attention, value_heads, preferred_element_type=jnp.float32
    )
    return mixed_rows.reshape(query_heads.shape[0], -1)


def backward_block(query_heads, grad_heads, key_rows, value_rows, weight, score_scale):
    col_count = key_rows.shape[0]
    row_count = query_heads.shape[0]
    key_heads = key_rows.reshape(col_count, HEADS, -1)
    value_heads = value_rows.reshape(col_count, HEADS, -1)
    scores = (
        jnp.einsum("ihd,jhd->hij", query_heads, key_heads, preferred_element_type=jnp.float32)
        * score_scale
    )
    sigmoid_scores = jax.nn.sigmoid(scores)
    attention = (scores * sigmoid_scores * weight[None]).astype(jnp.bfloat16)
    grad_attention = jnp.einsum(
        "ihd,jhd->hij", grad_heads, value_heads, preferred_element_type=jnp.float32
    )
    grad_scores = (grad_attention * weight[None] * silu_grad(scores, sigmoid_scores)).astype(
        jnp.bfloat16
    )
    grad_values = jnp.einsum(
        "hij,ihd->jhd", attention, grad_heads, preferred_element_type=jnp.float32
    ).reshape(col_count, -1)
    grad_query = (
        jnp.einsum(
            "hij,jhd->ihd", grad_scores, key_heads, preferred_element_type=jnp.float32
        ).reshape(row_count, -1)
        * score_scale
    )
    grad_keys = (
        jnp.einsum(
            "hij,ihd->jhd", grad_scores, query_heads, preferred_element_type=jnp.float32
        ).reshape(col_count, -1)
        * score_scale
    )
    return (grad_query, grad_keys, grad_values)


def pack_rows(grad_events, shards, table_rows, data_size, loop_size, capacity):
    row_count, model_width = grad_events.shape
    slot_count = data_size * loop_size * capacity
    earlier = jnp.arange(row_count)[None, :] < jnp.arange(row_count)[:, None]
    matches = (shards[:, None] == shards[None, :]) & earlier
    slot_rank = jnp.sum(matches.astype(jnp.int32), axis=1)
    target = shards * capacity + slot_rank
    onehot = jnp.arange(slot_count, dtype=jnp.int32)[:, None] == target[None, :]
    packed = jnp.dot(
        onehot.astype(jnp.float32),
        grad_events,
        precision=lax.Precision.HIGHEST,
        preferred_element_type=jnp.float32,
    )
    labels = jnp.sum(jnp.where(onehot, table_rows[None, :] + 1, 0), axis=1) - 1
    return (
        packed.reshape(data_size, loop_size, capacity, model_width),
        labels.reshape(data_size, loop_size, capacity),
    )


def merge_rows(received, row_marks):
    model_width = received.shape[-1]
    flat_rows = received.reshape(-1, model_width)
    flat_marks = row_marks.reshape(-1)
    matches = ((flat_marks[:, None] == flat_marks[None, :]) & (flat_marks[None, :] >= 0)).astype(
        jnp.float32
    )
    return jnp.dot(
        matches, flat_rows, precision=lax.Precision.HIGHEST, preferred_element_type=jnp.float32
    )


def body(
    events,
    out_grad,
    proj_weight,
    out_weight,
    lengths,
    tile_mask,
    quotient_shard,
    quotient_row,
    remainder_shard,
    remainder_row,
):
    row_count, model_width = events.shape
    loop_size = lax.axis_size("ctx")
    data_size = lax.axis_size("dp")
    loop_place = lax.axis_index("ctx")
    longest = float(row_count * loop_size // 2)
    score_scale = 1.0 / math.sqrt(model_width // HEADS)
    history = lengths[0]
    row_start = loop_place * row_count
    projected = jnp.dot(events, proj_weight, preferred_element_type=jnp.float32)
    sigmoid_proj = jax.nn.sigmoid(projected)
    activated = (projected * sigmoid_proj).astype(jnp.bfloat16)
    gate_rows = activated[:, :model_width].astype(jnp.float32)
    value_rows = activated[:, model_width : 2 * model_width]
    query_rows = activated[:, 2 * model_width : 3 * model_width]
    key_rows = activated[:, 3 * model_width :]
    query_heads = query_rows.reshape(row_count, HEADS, -1)
    empty_rows = jnp.zeros((row_count, model_width), jnp.float32)

    def forward_turn(turn_index, state):
        running, key_block, value_block = state
        offset_row = (loop_place - turn_index) % loop_size * row_count
        weight = visible_weight(
            history, tile_mask, row_start, row_count, offset_row, row_count, longest
        )
        running = running + guarded(
            weight,
            lambda: forward_block(query_heads, key_block, value_block, weight, score_scale),
            empty_rows,
        )
        key_next, value_next = passed_along((key_block, value_block), "ctx", 1)
        return (running, key_next, value_next)

    mixed_rows, key_spent, value_spent = lax.fori_loop(
        0, loop_size, forward_turn, (empty_rows, key_rows, value_rows)
    )
    row_mean = jnp.mean(mixed_rows, axis=1, keepdims=True)
    centered = mixed_rows - row_mean
    inv_scale = lax.rsqrt(jnp.mean(centered * centered, axis=1, keepdims=True) + EPSILON)
    normed = centered * inv_scale
    gated_rows = (normed * gate_rows).astype(jnp.bfloat16)
    out_weight_term = jnp.einsum(
        "td,te->de", gated_rows, out_grad, preferred_element_type=jnp.float32
    )
    grad_gated = jnp.einsum("te,de->td", out_grad, out_weight, preferred_element_type=jnp.float32)
    grad_normed = grad_gated * gate_rows
    grad_gate = grad_gated * normed
    grad_mixed = (
        inv_scale
        * (
            grad_normed
            - jnp.mean(grad_normed, axis=1, keepdims=True)
            - normed * jnp.mean(grad_normed * normed, axis=1, keepdims=True)
        )
    ).astype(jnp.bfloat16)
    grad_heads = grad_mixed.reshape(row_count, HEADS, -1)
    empty_triple = (empty_rows, empty_rows, empty_rows)

    def cycle_turn(turn_index, state):
        grad_query, key_block, value_block, key_grad_block, value_grad_block = state
        offset_row = (loop_place - turn_index) % loop_size * row_count
        weight = visible_weight(
            history, tile_mask, row_start, row_count, offset_row, row_count, longest
        )
        query_add, key_add, value_add = guarded(
            weight,
            lambda: backward_block(
                query_heads, grad_heads, key_block, value_block, weight, score_scale
            ),
            empty_triple,
        )
        key_next, value_next = passed_along((key_block, value_block), "ctx", 1)
        key_grad_next, value_grad_next = from_behind(
            (key_grad_block + key_add, value_grad_block + value_add), "ctx", 1
        )
        return (grad_query + query_add, key_next, value_next, key_grad_next, value_grad_next)

    grad_query, key_back, value_back, grad_keys, grad_values = lax.fori_loop(
        0, loop_size, cycle_turn, (empty_rows, key_rows, value_rows, empty_rows, empty_rows)
    )
    grad_projected = (
        jnp.concatenate([grad_gate, grad_values, grad_query, grad_keys], axis=1)
        * silu_grad(projected, sigmoid_proj)
    ).astype(jnp.bfloat16)
    grad_events = out_grad.astype(jnp.float32) + jnp.einsum(
        "tf,df->td", grad_projected, proj_weight, preferred_element_type=jnp.float32
    )
    proj_weight_term = jnp.einsum(
        "td,tf->df", events, grad_projected, preferred_element_type=jnp.float32
    )
    proj_weight_grad, out_weight_grad = lax.psum((proj_weight_term, out_weight_term), ("dp", "ctx"))
    devices = data_size * loop_size
    capacity = max(2, 3 * row_count // (2 * devices))
    quotient_buffer, quotient_labels = pack_rows(
        grad_events, quotient_shard, quotient_row, data_size, loop_size, capacity
    )
    remainder_buffer, remainder_labels = pack_rows(
        grad_events, remainder_shard, remainder_row, data_size, loop_size, capacity
    )
    quotient_in, remainder_in, quotient_marks, remainder_marks = (
        lax.all_to_all(
            lax.all_to_all(quotient_buffer, "dp", split_axis=0, concat_axis=0, tiled=True),
            "ctx",
            split_axis=1,
            concat_axis=1,
            tiled=True,
        ),
        lax.all_to_all(
            lax.all_to_all(remainder_buffer, "dp", split_axis=0, concat_axis=0, tiled=True),
            "ctx",
            split_axis=1,
            concat_axis=1,
            tiled=True,
        ),
        lax.all_to_all(
            lax.all_to_all(quotient_labels, "dp", split_axis=0, concat_axis=0, tiled=True),
            "ctx",
            split_axis=1,
            concat_axis=1,
            tiled=True,
        ),
        lax.all_to_all(
            lax.all_to_all(remainder_labels, "dp", split_axis=0, concat_axis=0, tiled=True),
            "ctx",
            split_axis=1,
            concat_axis=1,
            tiled=True,
        ),
    )
    quotient_grads = merge_rows(quotient_in, quotient_marks)
    remainder_grads = merge_rows(remainder_in, remainder_marks)
    return (quotient_grads, remainder_grads, proj_weight_grad, out_weight_grad)


F32 = jnp.float32
BF16 = jnp.bfloat16
MESH = pl.DeviceIdType.MESH
BLOCK = 32
WIDTH = 512


def dot_rows(a, b):
    return lax.dot_general(a, b, (((1,), (1,)), ((), ())), preferred_element_type=F32)


def dot_first(a, b):
    return lax.dot_general(a, b, (((0,), (0,)), ((), ())), preferred_element_type=F32)


def sigmoid_of(x):
    return 0.5 * jnp.tanh(0.5 * x) + 0.5


def layer_kernel(
    data_size, lengths_ref, tiles_ref, ev_own, og_own, weight_ref, out_weight_ref,
    shards_ref, rows_ref, got_ref, sum_ref,
    ev, og, act, dact, att, slope, mixed, gm, mask, gp, gated, pack, chosen_slots, slot_numbers,
    part_a, part_b, part_c, income_a, income_b, income_c, outgo_a, outgo_b, outgo_c,
    totals_a, totals_b, totals_c,
    local_sem, ctx_send, ctx_recv, row_send, row_recv, red_send, red_recv, all_send, all_recv,
):
    half, width = ev_own.shape
    full = 2 * half
    data = lax.axis_index("dp")
    place = lax.axis_index("ctx")
    me = data * 2 + place
    devices = data_size * 2
    steps = data_size.bit_length() - 1
    own = pl.multiple_of(place * half, half)
    far = pl.multiple_of((1 - place) * half, half)
    mine = pl.ds(own, half)
    across_x = (data, 1 - place)
    barrier = pltpu.get_barrier_semaphore()

    def other(k):
        to = lax.rem(me + k, devices)
        return to, (to // 2, lax.rem(to, 2))

    def remote(src, dst, send, recv, where):
        return pltpu.make_async_remote_copy(
            src_ref=src, dst_ref=dst, send_sem=send, recv_sem=recv, device_id=where,
            device_id_type=MESH,
        )

    @pl.loop(1, devices)
    def _(k):
        _, where = other(k)
        pl.semaphore_signal(barrier, inc=1, device_id=where, device_id_type=MESH)

    pl.semaphore_wait(barrier, devices - 1)
    ev_copy = remote(ev_own, ev.at[mine], ctx_send.at[0], ctx_recv.at[0], across_x)
    og_copy = remote(og_own, og.at[mine], ctx_send.at[1], ctx_recv.at[1], across_x)
    ev_copy.start()
    og_copy.start()
    ev[mine, :] = ev_own[...]
    og[mine, :] = og_own[...]

    def project(start):
        rows = pl.ds(start, half)

        @pl.loop(0, 4 * width // 256)
        def _(n):
            cols = pl.ds(pl.multiple_of(n * 256, 256), 256)
            projected = jnp.dot(ev[rows, :], weight_ref[:, cols], preferred_element_type=F32)
            sig = sigmoid_of(projected)
            act[rows, cols] = (projected * sig).astype(BF16)
            dact[rows, cols] = sig * (1.0 + projected * (1.0 - sig))

    project(own)

    ends = []
    total = jnp.int32(0)
    for k in range(lengths_ref.shape[1]):
        total = total + lengths_ref[0, k]
        ends.append(total)
    longest = float(full // 2)
    tiles = full // TILE
    mask[...] = jnp.zeros_like(mask)
    for a in range(tiles):
        row = a * TILE + lax.broadcasted_iota(jnp.int32, (TILE, TILE), 0)
        row_doc = sum((row >= e).astype(jnp.int32) for e in ends)
        for b in range(a + 1):
            col = b * TILE + lax.broadcasted_iota(jnp.int32, (TILE, TILE), 1)
            col_doc = sum((col >= e).astype(jnp.int32) for e in ends)
            keep = tiles_ref[a, b].astype(F32) / longest
            seen = (row_doc == col_doc) & (col <= row)
            mask[a * TILE : (a + 1) * TILE, b * TILE : (b + 1) * TILE] = jnp.where(seen, keep, 0.0)

    slots = pack.shape[0]
    capacity = 3 * half // (2 * (slots // BLOCK))
    early = lax.broadcasted_iota(jnp.int32, (half, half), 0) < lax.broadcasted_iota(
        jnp.int32, (half, half), 1
    )
    slot = lax.broadcasted_iota(jnp.int32, (slots, half), 0)
    spot = lax.broadcasted_iota(jnp.int32, (128, half), 0)
    onehot = jnp.zeros((slots, half), F32)
    numbers = jnp.zeros((slots, 128), F32)
    for t in range(2):
        shard = shards_ref[t : t + 1, :]
        across = jnp.broadcast_to(shard.astype(F32), (half, half))
        same = (jnp.transpose(across) == across) & early
        rank = jnp.sum(same.astype(F32), axis=0, keepdims=True).astype(jnp.int32)
        at = rank + t * capacity
        onehot = onehot + (slot == shard * BLOCK + at).astype(F32)
        number = rows_ref[t : t + 1, :]
        high = (number // 256 + 1).astype(F32)
        low = (number % 256).astype(F32)
        left = jnp.where(slot == shard * BLOCK + 2 * capacity, high, 0.0) + jnp.where(
            slot == shard * BLOCK + 2 * capacity + 1, low, 0.0
        )
        numbers = numbers + dot_rows(left.astype(BF16), (spot == at).astype(BF16))
    chosen_slots[...] = onehot.astype(BF16)
    slot_numbers[...] = numbers
    ev_copy.wait_recv()
    project(far)

    scale = 1.0 / math.sqrt(width // HEADS)
    head_width = width // HEADS
    lane = lax.broadcasted_iota(jnp.int32, (1, 128), 1) // head_width

    def pair_cols(base, p):
        return pl.ds(pl.multiple_of(base * width + p * 128, 128), 128)

    def only(x, h):
        return jnp.where(lane == h, x, jnp.zeros_like(x))

    blocks = ((0, half), (half, full))

    @pl.loop(0, width // 128)
    def _(p):
        q = (act[:, pair_cols(2, p)].astype(F32) * scale).astype(BF16)
        k = act[:, pair_cols(3, p)]
        v = act[:, pair_cols(1, p)]
        for lo, hi in blocks:
            total = jnp.zeros((half, 128), F32)
            for h in range(2):
                scores = dot_rows(only(q[lo:hi], h), k[:hi])
                sig = sigmoid_of(scores)
                w = mask[lo:hi, :hi]
                a = (scores * sig * w).astype(BF16)
                att[p * 2 + h, lo:hi, :hi] = a
                slope[p * 2 + h, lo:hi, :hi] = w * sig * (1.0 + scores * (1.0 - sig))
                total = total + jnp.dot(a, only(v[:hi], h), preferred_element_type=F32)
            mixed[lo:hi, pl.ds(pl.multiple_of(p * 128, 128), 128)] = total

    og_copy.wait_recv()

    @pl.loop(0, full // 128)
    def _(r):
        rows = pl.ds(pl.multiple_of(r * 128, 128), 128)
        m = mixed[rows, :]
        centered = m - jnp.mean(m, axis=1, keepdims=True)
        inv = lax.rsqrt(jnp.mean(centered * centered, axis=1, keepdims=True) + EPSILON)
        normed = centered * inv
        gate = act[rows, :width].astype(F32)
        gated[rows, :] = (normed * gate).astype(BF16)
        grad_gated = dot_rows(og[rows, :], out_weight_ref[...])
        grad_normed = grad_gated * gate
        gp[rows, :width] = (grad_gated * normed * dact[rows, :width]).astype(BF16)
        gm[rows, :] = (
            inv
            * (
                grad_normed
                - jnp.mean(grad_normed, axis=1, keepdims=True)
                - normed * jnp.mean(grad_normed * normed, axis=1, keepdims=True)
            )
        ).astype(BF16)

    def back_pair(p):
        q = (act[:, pair_cols(2, p)].astype(F32) * scale).astype(BF16)
        k = act[:, pair_cols(3, p)]
        v = act[:, pair_cols(1, p)]
        g = gm[:, pair_cols(0, p)]
        dv = [jnp.zeros((half, 128), F32)] * 2
        dk = [jnp.zeros((half, 128), F32)] * 2
        dq = [jnp.zeros((half, 128), F32)] * 2
        for h in range(2):
            kh, gh, qh = only(k, h), only(g, h), only(q, h)
            for n, (lo, hi) in enumerate(blocks):
                grad_att = dot_rows(gh[lo:hi], v[:hi])
                gs = (grad_att * slope[p * 2 + h, lo:hi, :hi]).astype(BF16)
                dq[n] = dq[n] + jnp.dot(gs, kh[:hi], preferred_element_type=F32)
                a = att[p * 2 + h, lo:hi, :hi]
                for m in range(n + 1):
                    at = slice(m * half, (m + 1) * half)
                    dv[m] = dv[m] + dot_first(a[:, at], gh[lo:hi])
                    dk[m] = dk[m] + dot_first(gs[:, at], qh[lo:hi])
        for n, (lo, hi) in enumerate(blocks):
            for base, value in ((1, dv[n]), (2, dq[n] * scale), (3, dk[n])):
                cols = pair_cols(base, p)
                gp[lo:hi, cols] = (value * dact[lo:hi, cols]).astype(BF16)

    def bit(n):
        return lax.rem(data // (1 << n), 2)

    def toward(n):
        return (data + (1 - 2 * bit(n)) * (1 << n), place)

    height = half

    def travel(which, part, income, outgo, totals, left, last):
        wide = part.shape[1]
        columns = pl.ds(left, wide)

        def halving(n):
            size = height >> (n + 1)
            if n == 0:
                src = part.at[pl.ds(pl.multiple_of((1 - bit(0)) * size, size), size)]
            else:
                src = outgo.at[pl.ds(height - 2 * size, size)]
            dst = income.at[pl.ds(height - 2 * size, size)]
            return remote(src, dst, red_send.at[which, n], red_recv.at[which, n], toward(n))

        sent = [halving(0)]
        sent[0].start()
        yield
        offset = place * height
        for n in range(steps):
            size = height >> (n + 1)
            came = pl.ds(height - 2 * size, size)
            sent[n].wait_recv()
            kept = pl.ds(pl.multiple_of(bit(n) * size, size), size)
            held = part[kept, :].astype(F32) if n == 0 else totals[kept, :]
            held = held + income[came, :].astype(F32)
            offset = offset + bit(n) * size
            if n + 1 < steps:
                totals[:size, :] = held
                small = size // 2
                gone = pl.ds(pl.multiple_of((1 - bit(n + 1)) * small, small), small)
                outgo[pl.ds(height - 2 * small, small), :] = totals[gone, :].astype(BF16)
                sent.append(halving(n + 1))
                sent[-1].start()
                yield
            else:
                sum_ref[pl.ds(pl.multiple_of(offset, size), size), columns] = held.astype(BF16)

        count = [0]

        def spread(start, size, where):
            rows = sum_ref.at[pl.ds(pl.multiple_of(start, 16), size), columns]
            n = count[0]
            count[0] += 1
            copy = remote(rows, rows, all_send.at[which, n], all_recv.at[which, n], where)
            copy.start()
            sent.append(copy)
            return copy

        size = height >> steps
        for n in range(steps - 1, 1, -1):
            copy = spread(offset, size, toward(n))
            yield
            copy.wait_recv()
            offset = offset - bit(n) * size
            size = 2 * size
        mirror = (1 - 2 * place) * height
        if last == "x":
            copy = spread(offset, size, toward(1))
            yield
            copy.wait_recv()
            offset = offset - bit(1) * size
            size = 2 * size
            first = spread(offset, size, across_x)
            near = spread(offset, size, toward(0))
            yield
            first.wait_recv()
            back = spread(offset + mirror, size, toward(0))
            yield
            near.wait_recv()
            back.wait_recv()
        else:
            first = spread(offset, size, across_x)
            second = spread(offset, size, toward(1))
            yield
            first.wait_recv()
            third = spread(offset + mirror, size, toward(1))
            yield
            second.wait_recv()
            offset = offset - bit(1) * size
            size = 2 * size
            near = spread(offset, size, toward(0))
            third.wait_recv()
            back = spread(offset + mirror, size, toward(0))
            yield
            near.wait_recv()
            back.wait_recv()
        for copy in sent:
            copy.wait_send()

    part_a[:, :width] = dot_first(gated[:, mine], og[...]).astype(BF16)
    ev_mine = ev[:, mine]
    part_a[:, width:] = dot_first(ev_mine, gp[:, :width]).astype(BF16)
    run_a = travel(0, part_a, income_a, outgo_a, totals_a, 0, "x")
    next(run_a)

    pairs = width // 128
    pl.loop(0, pairs // 2)(back_pair)
    next(run_a)
    pl.loop(pairs // 2, pairs)(back_pair)
    next(run_a)

    grad_events = (og_own[...].astype(F32) + dot_rows(gp[mine, :], weight_ref[...])).astype(BF16)
    packed = jnp.dot(chosen_slots[...], grad_events, preferred_element_type=F32)
    pack[:, :128] = (packed[:, :128] + slot_numbers[...]).astype(BF16)
    pack[:, 128:] = packed[:, 128:].astype(BF16)

    def row_copy(k):
        to, where = other(k)
        return remote(
            pack.at[pl.ds(pl.multiple_of(to * BLOCK, BLOCK), BLOCK)],
            got_ref.at[pl.ds(pl.multiple_of(me * BLOCK, BLOCK), BLOCK)],
            row_send.at[k],
            row_recv.at[k],
            where,
        )

    here = pl.ds(pl.multiple_of(me * BLOCK, BLOCK), BLOCK)
    local = pltpu.make_async_copy(pack.at[here], got_ref.at[here], local_sem)
    local.start()

    @pl.loop(1, devices)
    def _(k):
        row_copy(k).start()

    next(run_a)
    third = part_b.shape[1]
    part_b[...] = dot_first(ev_mine, gp[:, width : width + third]).astype(BF16)
    run_b = travel(1, part_b, income_b, outgo_b, totals_b, 2 * width, "y")
    next(run_b)
    part_c[...] = dot_first(ev_mine, gp[:, width + third :]).astype(BF16)
    run_c = travel(2, part_c, income_c, outgo_c, totals_c, 2 * width + third, "y")
    next(run_c)
    running = [run_a, run_b, run_c]
    while running:
        running = [run for run in running if next(run, "end") != "end"]

    ev_copy.wait_send()
    og_copy.wait_send()
    local.wait()

    @pl.loop(1, devices)
    def _(k):
        copy = row_copy(k)
        copy.wait_send()
        copy.wait_recv()


def pair_body(
    events, out_grad, proj_weight, out_weight, lengths, tile_mask,
    quotient_shard, quotient_row, remainder_shard, remainder_row,
):
    half, width = events.shape
    data_size = lax.axis_size("dp")
    devices = 2 * data_size
    capacity = 3 * half // (2 * devices)
    full = 2 * half
    shards = jnp.stack([quotient_shard, remainder_shard])
    numbers = jnp.stack([quotient_row, remainder_row])
    vmem = pl.BlockSpec(memory_space=pltpu.VMEM)
    smem = pl.BlockSpec(memory_space=pltpu.SMEM)
    steps = data_size.bit_length() - 1
    wides = (2 * width, 3 * width // 2, 3 * width // 2)
    got, sums = pl.pallas_call(
        lambda *refs: layer_kernel(data_size, *refs),
        name="layer",
        out_shape=(
            jax.ShapeDtypeStruct((devices * BLOCK, width), BF16),
            jax.ShapeDtypeStruct((full, 5 * width), BF16),
        ),
        in_specs=[smem] * 2 + [vmem] * 6,
        out_specs=(vmem, vmem),
        scratch_shapes=[
            pltpu.VMEM((full, width), BF16),
            pltpu.VMEM((full, width), BF16),
            pltpu.VMEM((full, 4 * width), BF16),
            pltpu.VMEM((full, 4 * width), F32),
            pltpu.VMEM((HEADS, full, full), BF16),
            pltpu.VMEM((HEADS, full, full), F32),
            pltpu.VMEM((full, width), F32),
            pltpu.VMEM((full, width), BF16),
            pltpu.VMEM((full, full), F32),
            pltpu.VMEM((full, 4 * width), BF16),
            pltpu.VMEM((full, width), BF16),
            pltpu.VMEM((devices * BLOCK, width), BF16),
            pltpu.VMEM((devices * BLOCK, half), BF16),
            pltpu.VMEM((devices * BLOCK, 128), F32),
            *[pltpu.VMEM((half, wide), BF16) for wide in wides],
            *[pltpu.VMEM((half, wide), BF16) for wide in wides],
            *[pltpu.VMEM((half, wide), BF16) for wide in wides],
            *[pltpu.VMEM((half // 2, wide), F32) for wide in wides],
            pltpu.SemaphoreType.DMA,
            pltpu.SemaphoreType.DMA((2,)),
            pltpu.SemaphoreType.DMA((2,)),
            pltpu.SemaphoreType.DMA((devices,)),
            pltpu.SemaphoreType.DMA((devices,)),
            pltpu.SemaphoreType.DMA((3, steps)),
            pltpu.SemaphoreType.DMA((3, steps)),
            pltpu.SemaphoreType.DMA((3, steps + 3)),
            pltpu.SemaphoreType.DMA((3, steps + 3)),
        ],
        compiler_params=pltpu.CompilerParams(
            collective_id=0, has_side_effects=True, vmem_limit_bytes=56 * 2**20
        ),
        cost_estimate=pl.CostEstimate(
            flops=10 * 10**9, bytes_accessed=8 * 2**20, transcendentals=4 * 10**6
        ),
    )(
        lengths, tile_mask, events, out_grad, proj_weight, out_weight, shards, numbers,
    )
    blocks = got.reshape(devices, BLOCK, width)
    head = blocks[:, 2 * capacity : 2 * capacity + 2, : 2 * capacity].astype(jnp.int32)
    marks = jnp.where(head[:, 0] > 0, (head[:, 0] - 1) * 256 + head[:, 1], -1)
    blank = jnp.full((devices, BLOCK), -1, jnp.int32)
    grads = []
    for t in range(2):
        mine = marks[:, t * capacity : (t + 1) * capacity]
        keys = lax.dynamic_update_slice(blank, mine, (0, t * capacity)).reshape(-1)
        slots = mine.reshape(-1)
        matches = (slots[:, None] == keys[None, :]) & (keys[None, :] >= 0)
        grads.append(jnp.dot(matches.astype(BF16), got, preferred_element_type=F32))
    return (
        grads[0],
        grads[1],
        sums[:, width:].astype(F32),
        sums[:, :width].astype(F32),
    )


def pair_fits(mesh):
    data_size, loop_size = mesh.shape["dp"], mesh.shape["ctx"]
    return loop_size == 2 and data_size == 16


def solution(mesh):
    chosen = pair_body if pair_fits(mesh) else body
    in_specs = (
        P(("dp", "ctx"), None),
        P(("dp", "ctx"), None),
        P(),
        P(),
        P("dp", None),
        P("dp", None),
        P(("dp", "ctx")),
        P(("dp", "ctx")),
        P(("dp", "ctx")),
        P(("dp", "ctx")),
    )
    out_specs = (P(("dp", "ctx"), None), P(("dp", "ctx"), None), P(), P())
    return jax.shard_map(chosen, mesh=mesh, in_specs=in_specs, out_specs=out_specs, check_vma=False)
```

```python
import math

import jax
import jax.numpy as jnp
from jax import lax
from jax.experimental import pallas as pl
from jax.experimental.pallas import tpu as pltpu
from jax.sharding import PartitionSpec as P

HEADS = 8
TILE = 128


EPSILON = 1e-05


def passed_along(shard, axis, by):
    count = lax.axis_size(axis)
    pairs = [(i, i + by) for i in range(count) if 0 <= i + by < count]
    return lax.ppermute(shard, axis, pairs)


def from_behind(shard, axis, by):
    count = lax.axis_size(axis)
    return lax.ppermute(shard, axis, [(i, (i + by) % count) for i in range(count)])


def silu_grad(value, sigma):
    return sigma * (1.0 + value * (1.0 - sigma))


def visible_weight(history, tile_table, row_start, row_count, col_start, col_count, longest):
    row_pos = row_start + jnp.arange(row_count, dtype=jnp.int32)
    col_pos = col_start + jnp.arange(col_count, dtype=jnp.int32)
    doc_ends = jnp.cumsum(history)
    row_doc = jnp.sum((row_pos[:, None] >= doc_ends[None, :]).astype(jnp.int32), axis=1)
    col_doc = jnp.sum((col_pos[:, None] >= doc_ends[None, :]).astype(jnp.int32), axis=1)
    tile_ids = jnp.arange(tile_table.shape[0], dtype=jnp.int32)
    row_tiles = (row_pos[:, None] // TILE == tile_ids[None, :]).astype(jnp.float32)
    col_tiles = (col_pos[:, None] // TILE == tile_ids[None, :]).astype(jnp.float32)
    tile_rows = jnp.dot(row_tiles, tile_table.astype(jnp.float32), precision=lax.Precision.HIGHEST)
    tile_full = jnp.dot(tile_rows, col_tiles.T, precision=lax.Precision.HIGHEST)
    visible = (
        (row_doc[:, None] == col_doc[None, :])
        & (col_pos[None, :] <= row_pos[:, None])
        & (tile_full > 0.5)
    )
    return visible.astype(jnp.float32) / longest


def guarded(weight, compute, empty_result):
    return lax.cond(jnp.any(weight > 0.0), compute, lambda: empty_result)


def forward_block(query_heads, key_rows, value_rows, weight, score_scale):
    col_count = key_rows.shape[0]
    key_heads = key_rows.reshape(col_count, HEADS, -1)
    value_heads = value_rows.reshape(col_count, HEADS, -1)
    scores = (
        jnp.einsum("ihd,jhd->hij", query_heads, key_heads, preferred_element_type=jnp.float32)
        * score_scale
    )
    attention = (scores * jax.nn.sigmoid(scores) * weight[None]).astype(jnp.bfloat16)
    mixed_rows = jnp.einsum(
        "hij,jhd->ihd", attention, value_heads, preferred_element_type=jnp.float32
    )
    return mixed_rows.reshape(query_heads.shape[0], -1)


def backward_block(query_heads, grad_heads, key_rows, value_rows, weight, score_scale):
    col_count = key_rows.shape[0]
    row_count = query_heads.shape[0]
    key_heads = key_rows.reshape(col_count, HEADS, -1)
    value_heads = value_rows.reshape(col_count, HEADS, -1)
    scores = (
        jnp.einsum("ihd,jhd->hij", query_heads, key_heads, preferred_element_type=jnp.float32)
        * score_scale
    )
    sigmoid_scores = jax.nn.sigmoid(scores)
    attention = (scores * sigmoid_scores * weight[None]).astype(jnp.bfloat16)
    grad_attention = jnp.einsum(
        "ihd,jhd->hij", grad_heads, value_heads, preferred_element_type=jnp.float32
    )
    grad_scores = (grad_attention * weight[None] * silu_grad(scores, sigmoid_scores)).astype(
        jnp.bfloat16
    )
    grad_values = jnp.einsum(
        "hij,ihd->jhd", attention, grad_heads, preferred_element_type=jnp.float32
    ).reshape(col_count, -1)
    grad_query = (
        jnp.einsum(
            "hij,jhd->ihd", grad_scores, key_heads, preferred_element_type=jnp.float32
        ).reshape(row_count, -1)
        * score_scale
    )
    grad_keys = (
        jnp.einsum(
            "hij,ihd->jhd", grad_scores, query_heads, preferred_element_type=jnp.float32
        ).reshape(col_count, -1)
        * score_scale
    )
    return (grad_query, grad_keys, grad_values)


def pack_rows(grad_events, shards, table_rows, data_size, loop_size, capacity):
    row_count, model_width = grad_events.shape
    slot_count = data_size * loop_size * capacity
    earlier = jnp.arange(row_count)[None, :] < jnp.arange(row_count)[:, None]
    matches = (shards[:, None] == shards[None, :]) & earlier
    slot_rank = jnp.sum(matches.astype(jnp.int32), axis=1)
    target = shards * capacity + slot_rank
    onehot = jnp.arange(slot_count, dtype=jnp.int32)[:, None] == target[None, :]
    packed = jnp.dot(
        onehot.astype(jnp.float32),
        grad_events,
        precision=lax.Precision.HIGHEST,
        preferred_element_type=jnp.float32,
    )
    labels = jnp.sum(jnp.where(onehot, table_rows[None, :] + 1, 0), axis=1) - 1
    return (
        packed.reshape(data_size, loop_size, capacity, model_width),
        labels.reshape(data_size, loop_size, capacity),
    )


def merge_rows(received, row_marks):
    model_width = received.shape[-1]
    flat_rows = received.reshape(-1, model_width)
    flat_marks = row_marks.reshape(-1)
    matches = ((flat_marks[:, None] == flat_marks[None, :]) & (flat_marks[None, :] >= 0)).astype(
        jnp.float32
    )
    return jnp.dot(
        matches, flat_rows, precision=lax.Precision.HIGHEST, preferred_element_type=jnp.float32
    )


def body(
    events,
    out_grad,
    proj_weight,
    out_weight,
    lengths,
    tile_mask,
    quotient_shard,
    quotient_row,
    remainder_shard,
    remainder_row,
):
    row_count, model_width = events.shape
    loop_size = lax.axis_size("ctx")
    data_size = lax.axis_size("dp")
    loop_place = lax.axis_index("ctx")
    longest = float(row_count * loop_size // 2)
    score_scale = 1.0 / math.sqrt(model_width // HEADS)
    history = lengths[0]
    row_start = loop_place * row_count
    projected = jnp.dot(events, proj_weight, preferred_element_type=jnp.float32)
    sigmoid_proj = jax.nn.sigmoid(projected)
    activated = (projected * sigmoid_proj).astype(jnp.bfloat16)
    gate_rows = activated[:, :model_width].astype(jnp.float32)
    value_rows = activated[:, model_width : 2 * model_width]
    query_rows = activated[:, 2 * model_width : 3 * model_width]
    key_rows = activated[:, 3 * model_width :]
    query_heads = query_rows.reshape(row_count, HEADS, -1)
    empty_rows = jnp.zeros((row_count, model_width), jnp.float32)

    def forward_turn(turn_index, state):
        running, key_block, value_block = state
        offset_row = (loop_place - turn_index) % loop_size * row_count
        weight = visible_weight(
            history, tile_mask, row_start, row_count, offset_row, row_count, longest
        )
        running = running + guarded(
            weight,
            lambda: forward_block(query_heads, key_block, value_block, weight, score_scale),
            empty_rows,
        )
        key_next, value_next = passed_along((key_block, value_block), "ctx", 1)
        return (running, key_next, value_next)

    mixed_rows, key_spent, value_spent = lax.fori_loop(
        0, loop_size, forward_turn, (empty_rows, key_rows, value_rows)
    )
    row_mean = jnp.mean(mixed_rows, axis=1, keepdims=True)
    centered = mixed_rows - row_mean
    inv_scale = lax.rsqrt(jnp.mean(centered * centered, axis=1, keepdims=True) + EPSILON)
    normed = centered * inv_scale
    gated_rows = (normed * gate_rows).astype(jnp.bfloat16)
    out_weight_term = jnp.einsum(
        "td,te->de", gated_rows, out_grad, preferred_element_type=jnp.float32
    )
    grad_gated = jnp.einsum("te,de->td", out_grad, out_weight, preferred_element_type=jnp.float32)
    grad_normed = grad_gated * gate_rows
    grad_gate = grad_gated * normed
    grad_mixed = (
        inv_scale
        * (
            grad_normed
            - jnp.mean(grad_normed, axis=1, keepdims=True)
            - normed * jnp.mean(grad_normed * normed, axis=1, keepdims=True)
        )
    ).astype(jnp.bfloat16)
    grad_heads = grad_mixed.reshape(row_count, HEADS, -1)
    empty_triple = (empty_rows, empty_rows, empty_rows)

    def cycle_turn(turn_index, state):
        grad_query, key_block, value_block, key_grad_block, value_grad_block = state
        offset_row = (loop_place - turn_index) % loop_size * row_count
        weight = visible_weight(
            history, tile_mask, row_start, row_count, offset_row, row_count, longest
        )
        query_add, key_add, value_add = guarded(
            weight,
            lambda: backward_block(
                query_heads, grad_heads, key_block, value_block, weight, score_scale
            ),
            empty_triple,
        )
        key_next, value_next = passed_along((key_block, value_block), "ctx", 1)
        key_grad_next, value_grad_next = from_behind(
            (key_grad_block + key_add, value_grad_block + value_add), "ctx", 1
        )
        return (grad_query + query_add, key_next, value_next, key_grad_next, value_grad_next)

    grad_query, key_back, value_back, grad_keys, grad_values = lax.fori_loop(
        0, loop_size, cycle_turn, (empty_rows, key_rows, value_rows, empty_rows, empty_rows)
    )
    grad_projected = (
        jnp.concatenate([grad_gate, grad_values, grad_query, grad_keys], axis=1)
        * silu_grad(projected, sigmoid_proj)
    ).astype(jnp.bfloat16)
    grad_events = out_grad.astype(jnp.float32) + jnp.einsum(
        "tf,df->td", grad_projected, proj_weight, preferred_element_type=jnp.float32
    )
    proj_weight_term = jnp.einsum(
        "td,tf->df", events, grad_projected, preferred_element_type=jnp.float32
    )
    proj_weight_grad, out_weight_grad = lax.psum((proj_weight_term, out_weight_term), ("dp", "ctx"))
    devices = data_size * loop_size
    capacity = max(2, 3 * row_count // (2 * devices))
    quotient_buffer, quotient_labels = pack_rows(
        grad_events, quotient_shard, quotient_row, data_size, loop_size, capacity
    )
    remainder_buffer, remainder_labels = pack_rows(
        grad_events, remainder_shard, remainder_row, data_size, loop_size, capacity
    )
    quotient_in, remainder_in, quotient_marks, remainder_marks = (
        lax.all_to_all(
            lax.all_to_all(quotient_buffer, "dp", split_axis=0, concat_axis=0, tiled=True),
            "ctx",
            split_axis=1,
            concat_axis=1,
            tiled=True,
        ),
        lax.all_to_all(
            lax.all_to_all(remainder_buffer, "dp", split_axis=0, concat_axis=0, tiled=True),
            "ctx",
            split_axis=1,
            concat_axis=1,
            tiled=True,
        ),
        lax.all_to_all(
            lax.all_to_all(quotient_labels, "dp", split_axis=0, concat_axis=0, tiled=True),
            "ctx",
            split_axis=1,
            concat_axis=1,
            tiled=True,
        ),
        lax.all_to_all(
            lax.all_to_all(remainder_labels, "dp", split_axis=0, concat_axis=0, tiled=True),
            "ctx",
            split_axis=1,
            concat_axis=1,
            tiled=True,
        ),
    )
    quotient_grads = merge_rows(quotient_in, quotient_marks)
    remainder_grads = merge_rows(remainder_in, remainder_marks)
    return (quotient_grads, remainder_grads, proj_weight_grad, out_weight_grad)


F32 = jnp.float32
BF16 = jnp.bfloat16
MESH = pl.DeviceIdType.MESH
BLOCK = 32
WIDTH = 512


def dot_rows(a, b):
    return lax.dot_general(a, b, (((1,), (1,)), ((), ())), preferred_element_type=F32)


def dot_first(a, b):
    return lax.dot_general(a, b, (((0,), (0,)), ((), ())), preferred_element_type=F32)


def sigmoid_of(x):
    return 0.5 * jnp.tanh(0.5 * x) + 0.5


def layer_kernel(
    data_size, lengths_ref, tiles_ref, ev_own, og_own, weight_ref, out_weight_ref,
    shards_ref, rows_ref, got_ref, sum_ref,
    ev, og, act, dact, att, slope, mixed, gm, mask, gp, gated, pack, chosen_slots, slot_numbers,
    part_a, part_b, part_c, income_a, income_b, income_c, outgo_a, outgo_b, outgo_c,
    totals_a, totals_b, totals_c,
    local_sem, ctx_send, ctx_recv, row_send, row_recv, red_send, red_recv, all_send, all_recv,
):
    half, width = ev_own.shape
    full = 2 * half
    data = lax.axis_index("dp")
    place = lax.axis_index("ctx")
    me = data * 2 + place
    devices = data_size * 2
    steps = data_size.bit_length() - 1
    own = pl.multiple_of(place * half, half)
    far = pl.multiple_of((1 - place) * half, half)
    mine = pl.ds(own, half)
    across_x = (data, 1 - place)
    barrier = pltpu.get_barrier_semaphore()

    def other(k):
        to = lax.rem(me + k, devices)
        return to, (to // 2, lax.rem(to, 2))

    def remote(src, dst, send, recv, where):
        return pltpu.make_async_remote_copy(
            src_ref=src, dst_ref=dst, send_sem=send, recv_sem=recv, device_id=where,
            device_id_type=MESH,
        )

    @pl.loop(1, devices)
    def _(k):
        _, where = other(k)
        pl.semaphore_signal(barrier, inc=1, device_id=where, device_id_type=MESH)

    pl.semaphore_wait(barrier, devices - 1)
    ev_copy = remote(ev_own, ev.at[mine], ctx_send.at[0], ctx_recv.at[0], across_x)
    og_copy = remote(og_own, og.at[mine], ctx_send.at[1], ctx_recv.at[1], across_x)
    ev_copy.start()
    og_copy.start()
    ev[mine, :] = ev_own[...]
    og[mine, :] = og_own[...]

    def project(start):
        rows = pl.ds(start, half)

        @pl.loop(0, 4 * width // 256)
        def _(n):
            cols = pl.ds(pl.multiple_of(n * 256, 256), 256)
            projected = jnp.dot(ev[rows, :], weight_ref[:, cols], preferred_element_type=F32)
            sig = sigmoid_of(projected)
            act[rows, cols] = (projected * sig).astype(BF16)
            dact[rows, cols] = sig * (1.0 + projected * (1.0 - sig))

    project(own)

    ends = []
    total = jnp.int32(0)
    for k in range(lengths_ref.shape[1]):
        total = total + lengths_ref[0, k]
        ends.append(total)
    longest = float(full // 2)
    tiles = full // TILE
    mask[...] = jnp.zeros_like(mask)
    for a in range(tiles):
        row = a * TILE + lax.broadcasted_iota(jnp.int32, (TILE, TILE), 0)
        row_doc = sum((row >= e).astype(jnp.int32) for e in ends)
        for b in range(a + 1):
            col = b * TILE + lax.broadcasted_iota(jnp.int32, (TILE, TILE), 1)
            col_doc = sum((col >= e).astype(jnp.int32) for e in ends)
            keep = tiles_ref[a, b].astype(F32) / longest
            seen = (row_doc == col_doc) & (col <= row)
            mask[a * TILE : (a + 1) * TILE, b * TILE : (b + 1) * TILE] = jnp.where(seen, keep, 0.0)

    slots = pack.shape[0]
    capacity = 3 * half // (2 * (slots // BLOCK))
    early = lax.broadcasted_iota(jnp.int32, (half, half), 0) < lax.broadcasted_iota(
        jnp.int32, (half, half), 1
    )
    slot = lax.broadcasted_iota(jnp.int32, (slots, half), 0)
    spot = lax.broadcasted_iota(jnp.int32, (128, half), 0)
    onehot = jnp.zeros((slots, half), F32)
    numbers = jnp.zeros((slots, 128), F32)
    for t in range(2):
        shard = shards_ref[t : t + 1, :]
        across = jnp.broadcast_to(shard.astype(F32), (half, half))
        same = (jnp.transpose(across) == across) & early
        rank = jnp.sum(same.astype(F32), axis=0, keepdims=True).astype(jnp.int32)
        at = rank + t * capacity
        onehot = onehot + (slot == shard * BLOCK + at).astype(F32)
        number = rows_ref[t : t + 1, :]
        high = (number // 256 + 1).astype(F32)
        low = (number % 256).astype(F32)
        left = jnp.where(slot == shard * BLOCK + 2 * capacity, high, 0.0) + jnp.where(
            slot == shard * BLOCK + 2 * capacity + 1, low, 0.0
        )
        numbers = numbers + dot_rows(left.astype(BF16), (spot == at).astype(BF16))
    chosen_slots[...] = onehot.astype(BF16)
    slot_numbers[...] = numbers
    ev_copy.wait_recv()
    project(far)

    scale = 1.0 / math.sqrt(width // HEADS)
    head_width = width // HEADS
    lane = lax.broadcasted_iota(jnp.int32, (1, 128), 1) // head_width

    def pair_cols(base, p):
        return pl.ds(pl.multiple_of(base * width + p * 128, 128), 128)

    def only(x, h):
        return jnp.where(lane == h, x, jnp.zeros_like(x))

    blocks = ((0, half), (half, full))

    @pl.loop(0, width // 128)
    def _(p):
        q = (act[:, pair_cols(2, p)].astype(F32) * scale).astype(BF16)
        k = act[:, pair_cols(3, p)]
        v = act[:, pair_cols(1, p)]
        for lo, hi in blocks:
            total = jnp.zeros((half, 128), F32)
            for h in range(2):
                scores = dot_rows(only(q[lo:hi], h), k[:hi])
                sig = sigmoid_of(scores)
                w = mask[lo:hi, :hi]
                a = (scores * sig * w).astype(BF16)
                att[p * 2 + h, lo:hi, :hi] = a
                slope[p * 2 + h, lo:hi, :hi] = w * sig * (1.0 + scores * (1.0 - sig))
                total = total + jnp.dot(a, only(v[:hi], h), preferred_element_type=F32)
            mixed[lo:hi, pl.ds(pl.multiple_of(p * 128, 128), 128)] = total

    og_copy.wait_recv()

    @pl.loop(0, full // 128)
    def _(r):
        rows = pl.ds(pl.multiple_of(r * 128, 128), 128)
        m = mixed[rows, :]
        centered = m - jnp.mean(m, axis=1, keepdims=True)
        inv = lax.rsqrt(jnp.mean(centered * centered, axis=1, keepdims=True) + EPSILON)
        normed = centered * inv
        gate = act[rows, :width].astype(F32)
        gated[rows, :] = (normed * gate).astype(BF16)
        grad_gated = dot_rows(og[rows, :], out_weight_ref[...])
        grad_normed = grad_gated * gate
        gp[rows, :width] = (grad_gated * normed * dact[rows, :width]).astype(BF16)
        gm[rows, :] = (
            inv
            * (
                grad_normed
                - jnp.mean(grad_normed, axis=1, keepdims=True)
                - normed * jnp.mean(grad_normed * normed, axis=1, keepdims=True)
            )
        ).astype(BF16)

    def back_pair(p):
        q = (act[:, pair_cols(2, p)].astype(F32) * scale).astype(BF16)
        k = act[:, pair_cols(3, p)]
        v = act[:, pair_cols(1, p)]
        g = gm[:, pair_cols(0, p)]
        dv = [jnp.zeros((half, 128), F32)] * 2
        dk = [jnp.zeros((half, 128), F32)] * 2
        dq = [jnp.zeros((half, 128), F32)] * 2
        for h in range(2):
            kh, gh, qh = only(k, h), only(g, h), only(q, h)
            for n, (lo, hi) in enumerate(blocks):
                grad_att = dot_rows(gh[lo:hi], v[:hi])
                gs = (grad_att * slope[p * 2 + h, lo:hi, :hi]).astype(BF16)
                dq[n] = dq[n] + jnp.dot(gs, kh[:hi], preferred_element_type=F32)
                a = att[p * 2 + h, lo:hi, :hi]
                for m in range(n + 1):
                    at = slice(m * half, (m + 1) * half)
                    dv[m] = dv[m] + dot_first(a[:, at], gh[lo:hi])
                    dk[m] = dk[m] + dot_first(gs[:, at], qh[lo:hi])
        for n, (lo, hi) in enumerate(blocks):
            for base, value in ((1, dv[n]), (2, dq[n] * scale), (3, dk[n])):
                cols = pair_cols(base, p)
                gp[lo:hi, cols] = (value * dact[lo:hi, cols]).astype(BF16)

    def bit(n):
        return lax.rem(data // (1 << n), 2)

    def toward(n):
        return (data + (1 - 2 * bit(n)) * (1 << n), place)

    height = half

    def travel(which, part, income, outgo, totals, left, last):
        wide = part.shape[1]
        columns = pl.ds(left, wide)

        def halving(n):
            size = height >> (n + 1)
            if n == 0:
                src = part.at[pl.ds(pl.multiple_of((1 - bit(0)) * size, size), size)]
            else:
                src = outgo.at[pl.ds(height - 2 * size, size)]
            dst = income.at[pl.ds(height - 2 * size, size)]
            return remote(src, dst, red_send.at[which, n], red_recv.at[which, n], toward(n))

        sent = [halving(0)]
        sent[0].start()
        yield
        offset = place * height
        for n in range(steps):
            size = height >> (n + 1)
            came = pl.ds(height - 2 * size, size)
            sent[n].wait_recv()
            kept = pl.ds(pl.multiple_of(bit(n) * size, size), size)
            held = part[kept, :].astype(F32) if n == 0 else totals[kept, :]
            held = held + income[came, :].astype(F32)
            offset = offset + bit(n) * size
            if n + 1 < steps:
                totals[:size, :] = held
                small = size // 2
                gone = pl.ds(pl.multiple_of((1 - bit(n + 1)) * small, small), small)
                outgo[pl.ds(height - 2 * small, small), :] = totals[gone, :].astype(BF16)
                sent.append(halving(n + 1))
                sent[-1].start()
                yield
            else:
                sum_ref[pl.ds(pl.multiple_of(offset, size), size), columns] = held.astype(BF16)

        count = [0]

        def spread(start, size, where):
            rows = sum_ref.at[pl.ds(pl.multiple_of(start, 16), size), columns]
            n = count[0]
            count[0] += 1
            copy = remote(rows, rows, all_send.at[which, n], all_recv.at[which, n], where)
            copy.start()
            sent.append(copy)
            return copy

        size = height >> steps
        for n in range(steps - 1, 1, -1):
            copy = spread(offset, size, toward(n))
            yield
            copy.wait_recv()
            offset = offset - bit(n) * size
            size = 2 * size
        mirror = (1 - 2 * place) * height
        if last == "x":
            copy = spread(offset, size, toward(1))
            yield
            copy.wait_recv()
            offset = offset - bit(1) * size
            size = 2 * size
            first = spread(offset, size, across_x)
            near = spread(offset, size, toward(0))
            yield
            first.wait_recv()
            back = spread(offset + mirror, size, toward(0))
            yield
            near.wait_recv()
            back.wait_recv()
        else:
            first = spread(offset, size, across_x)
            second = spread(offset, size, toward(1))
            yield
            first.wait_recv()
            third = spread(offset + mirror, size, toward(1))
            yield
            second.wait_recv()
            offset = offset - bit(1) * size
            size = 2 * size
            near = spread(offset, size, toward(0))
            third.wait_recv()
            back = spread(offset + mirror, size, toward(0))
            yield
            near.wait_recv()
            back.wait_recv()
        for copy in sent:
            copy.wait_send()

    part_a[:, :width] = dot_first(gated[:, mine], og[...]).astype(BF16)
    ev_mine = ev[:, mine]
    part_a[:, width:] = dot_first(ev_mine, gp[:, :width]).astype(BF16)
    run_a = travel(0, part_a, income_a, outgo_a, totals_a, 0, "x")
    next(run_a)

    pairs = width // 128
    pl.loop(0, pairs // 2)(back_pair)
    next(run_a)
    pl.loop(pairs // 2, pairs)(back_pair)
    next(run_a)

    third = part_b.shape[1]
    part_b[...] = dot_first(ev_mine, gp[:, width : width + third]).astype(BF16)
    run_b = travel(1, part_b, income_b, outgo_b, totals_b, 2 * width, "y")
    next(run_b)
    next(run_a)
    part_c[...] = dot_first(ev_mine, gp[:, width + third :]).astype(BF16)
    run_c = travel(2, part_c, income_c, outgo_c, totals_c, 2 * width + third, "y")
    next(run_c)
    next(run_a)

    grad_events = (og_own[...].astype(F32) + dot_rows(gp[mine, :], weight_ref[...])).astype(BF16)
    packed = jnp.dot(chosen_slots[...], grad_events, preferred_element_type=F32)
    pack[:, :128] = (packed[:, :128] + slot_numbers[...]).astype(BF16)
    pack[:, 128:] = packed[:, 128:].astype(BF16)

    def row_copy(k):
        to, where = other(k)
        return remote(
            pack.at[pl.ds(pl.multiple_of(to * BLOCK, BLOCK), BLOCK)],
            got_ref.at[pl.ds(pl.multiple_of(me * BLOCK, BLOCK), BLOCK)],
            row_send.at[k],
            row_recv.at[k],
            where,
        )

    here = pl.ds(pl.multiple_of(me * BLOCK, BLOCK), BLOCK)
    local = pltpu.make_async_copy(pack.at[here], got_ref.at[here], local_sem)
    local.start()

    fourth = devices // 4
    turns = [[k for k in (g + fourth, g + 2 * fourth, g + 3 * fourth, g) if k] for g in range(fourth)]
    running = [run_a, run_b, run_c]
    while running or turns:
        for k in turns.pop(0) if turns else []:
            row_copy(k).start()
        running = [run for run in running if next(run, "end") != "end"]

    ev_copy.wait_send()
    og_copy.wait_send()
    local.wait()

    @pl.loop(1, devices)
    def _(k):
        copy = row_copy(k)
        copy.wait_send()
        copy.wait_recv()


def pair_body(
    events, out_grad, proj_weight, out_weight, lengths, tile_mask,
    quotient_shard, quotient_row, remainder_shard, remainder_row,
):
    half, width = events.shape
    data_size = lax.axis_size("dp")
    devices = 2 * data_size
    capacity = 3 * half // (2 * devices)
    full = 2 * half
    shards = jnp.stack([quotient_shard, remainder_shard])
    numbers = jnp.stack([quotient_row, remainder_row])
    vmem = pl.BlockSpec(memory_space=pltpu.VMEM)
    smem = pl.BlockSpec(memory_space=pltpu.SMEM)
    steps = data_size.bit_length() - 1
    wides = (2 * width, 3 * width // 2, 3 * width // 2)
    got, sums = pl.pallas_call(
        lambda *refs: layer_kernel(data_size, *refs),
        name="layer",
        out_shape=(
            jax.ShapeDtypeStruct((devices * BLOCK, width), BF16),
            jax.ShapeDtypeStruct((full, 5 * width), BF16),
        ),
        in_specs=[smem] * 2 + [vmem] * 6,
        out_specs=(vmem, vmem),
        scratch_shapes=[
            pltpu.VMEM((full, width), BF16),
            pltpu.VMEM((full, width), BF16),
            pltpu.VMEM((full, 4 * width), BF16),
            pltpu.VMEM((full, 4 * width), F32),
            pltpu.VMEM((HEADS, full, full), BF16),
            pltpu.VMEM((HEADS, full, full), F32),
            pltpu.VMEM((full, width), F32),
            pltpu.VMEM((full, width), BF16),
            pltpu.VMEM((full, full), F32),
            pltpu.VMEM((full, 4 * width), BF16),
            pltpu.VMEM((full, width), BF16),
            pltpu.VMEM((devices * BLOCK, width), BF16),
            pltpu.VMEM((devices * BLOCK, half), BF16),
            pltpu.VMEM((devices * BLOCK, 128), F32),
            *[pltpu.VMEM((half, wide), BF16) for wide in wides],
            *[pltpu.VMEM((half, wide), BF16) for wide in wides],
            *[pltpu.VMEM((half, wide), BF16) for wide in wides],
            *[pltpu.VMEM((half // 2, wide), F32) for wide in wides],
            pltpu.SemaphoreType.DMA,
            pltpu.SemaphoreType.DMA((2,)),
            pltpu.SemaphoreType.DMA((2,)),
            pltpu.SemaphoreType.DMA((devices,)),
            pltpu.SemaphoreType.DMA((devices,)),
            pltpu.SemaphoreType.DMA((3, steps)),
            pltpu.SemaphoreType.DMA((3, steps)),
            pltpu.SemaphoreType.DMA((3, steps + 3)),
            pltpu.SemaphoreType.DMA((3, steps + 3)),
        ],
        compiler_params=pltpu.CompilerParams(
            collective_id=0, has_side_effects=True, vmem_limit_bytes=56 * 2**20
        ),
        cost_estimate=pl.CostEstimate(
            flops=10 * 10**9, bytes_accessed=8 * 2**20, transcendentals=4 * 10**6
        ),
    )(
        lengths, tile_mask, events, out_grad, proj_weight, out_weight, shards, numbers,
    )
    blocks = got.reshape(devices, BLOCK, width)
    head = blocks[:, 2 * capacity : 2 * capacity + 2, : 2 * capacity].astype(jnp.int32)
    marks = jnp.where(head[:, 0] > 0, (head[:, 0] - 1) * 256 + head[:, 1], -1)
    blank = jnp.full((devices, BLOCK), -1, jnp.int32)
    grads = []
    for t in range(2):
        mine = marks[:, t * capacity : (t + 1) * capacity]
        keys = lax.dynamic_update_slice(blank, mine, (0, t * capacity)).reshape(-1)
        slots = mine.reshape(-1)
        matches = (slots[:, None] == keys[None, :]) & (keys[None, :] >= 0)
        grads.append(jnp.dot(matches.astype(BF16), got, preferred_element_type=F32))
    return (
        grads[0],
        grads[1],
        sums[:, width:].astype(F32),
        sums[:, :width].astype(F32),
    )


def pair_fits(mesh):
    data_size, loop_size = mesh.shape["dp"], mesh.shape["ctx"]
    return loop_size == 2 and data_size == 16


def solution(mesh):
    chosen = pair_body if pair_fits(mesh) else body
    in_specs = (
        P(("dp", "ctx"), None),
        P(("dp", "ctx"), None),
        P(),
        P(),
        P("dp", None),
        P("dp", None),
        P(("dp", "ctx")),
        P(("dp", "ctx")),
        P(("dp", "ctx")),
        P(("dp", "ctx")),
    )
    out_specs = (P(("dp", "ctx"), None), P(("dp", "ctx"), None), P(), P())
    return jax.shard_map(chosen, mesh=mesh, in_specs=in_specs, out_specs=out_specs, check_vma=False)
```

```python
import math

import jax
import jax.numpy as jnp
from jax import lax
from jax.experimental import pallas as pl
from jax.experimental.pallas import tpu as pltpu
from jax.sharding import PartitionSpec as P

HEADS = 8
TILE = 128


EPSILON = 1e-05


def passed_along(shard, axis, by):
    count = lax.axis_size(axis)
    pairs = [(i, i + by) for i in range(count) if 0 <= i + by < count]
    return lax.ppermute(shard, axis, pairs)


def from_behind(shard, axis, by):
    count = lax.axis_size(axis)
    return lax.ppermute(shard, axis, [(i, (i + by) % count) for i in range(count)])


def silu_grad(value, sigma):
    return sigma * (1.0 + value * (1.0 - sigma))


def visible_weight(history, tile_table, row_start, row_count, col_start, col_count, longest):
    row_pos = row_start + jnp.arange(row_count, dtype=jnp.int32)
    col_pos = col_start + jnp.arange(col_count, dtype=jnp.int32)
    doc_ends = jnp.cumsum(history)
    row_doc = jnp.sum((row_pos[:, None] >= doc_ends[None, :]).astype(jnp.int32), axis=1)
    col_doc = jnp.sum((col_pos[:, None] >= doc_ends[None, :]).astype(jnp.int32), axis=1)
    tile_ids = jnp.arange(tile_table.shape[0], dtype=jnp.int32)
    row_tiles = (row_pos[:, None] // TILE == tile_ids[None, :]).astype(jnp.float32)
    col_tiles = (col_pos[:, None] // TILE == tile_ids[None, :]).astype(jnp.float32)
    tile_rows = jnp.dot(row_tiles, tile_table.astype(jnp.float32), precision=lax.Precision.HIGHEST)
    tile_full = jnp.dot(tile_rows, col_tiles.T, precision=lax.Precision.HIGHEST)
    visible = (
        (row_doc[:, None] == col_doc[None, :])
        & (col_pos[None, :] <= row_pos[:, None])
        & (tile_full > 0.5)
    )
    return visible.astype(jnp.float32) / longest


def guarded(weight, compute, empty_result):
    return lax.cond(jnp.any(weight > 0.0), compute, lambda: empty_result)


def forward_block(query_heads, key_rows, value_rows, weight, score_scale):
    col_count = key_rows.shape[0]
    key_heads = key_rows.reshape(col_count, HEADS, -1)
    value_heads = value_rows.reshape(col_count, HEADS, -1)
    scores = (
        jnp.einsum("ihd,jhd->hij", query_heads, key_heads, preferred_element_type=jnp.float32)
        * score_scale
    )
    attention = (scores * jax.nn.sigmoid(scores) * weight[None]).astype(jnp.bfloat16)
    mixed_rows = jnp.einsum(
        "hij,jhd->ihd", attention, value_heads, preferred_element_type=jnp.float32
    )
    return mixed_rows.reshape(query_heads.shape[0], -1)


def backward_block(query_heads, grad_heads, key_rows, value_rows, weight, score_scale):
    col_count = key_rows.shape[0]
    row_count = query_heads.shape[0]
    key_heads = key_rows.reshape(col_count, HEADS, -1)
    value_heads = value_rows.reshape(col_count, HEADS, -1)
    scores = (
        jnp.einsum("ihd,jhd->hij", query_heads, key_heads, preferred_element_type=jnp.float32)
        * score_scale
    )
    sigmoid_scores = jax.nn.sigmoid(scores)
    attention = (scores * sigmoid_scores * weight[None]).astype(jnp.bfloat16)
    grad_attention = jnp.einsum(
        "ihd,jhd->hij", grad_heads, value_heads, preferred_element_type=jnp.float32
    )
    grad_scores = (grad_attention * weight[None] * silu_grad(scores, sigmoid_scores)).astype(
        jnp.bfloat16
    )
    grad_values = jnp.einsum(
        "hij,ihd->jhd", attention, grad_heads, preferred_element_type=jnp.float32
    ).reshape(col_count, -1)
    grad_query = (
        jnp.einsum(
            "hij,jhd->ihd", grad_scores, key_heads, preferred_element_type=jnp.float32
        ).reshape(row_count, -1)
        * score_scale
    )
    grad_keys = (
        jnp.einsum(
            "hij,ihd->jhd", grad_scores, query_heads, preferred_element_type=jnp.float32
        ).reshape(col_count, -1)
        * score_scale
    )
    return (grad_query, grad_keys, grad_values)


def pack_rows(grad_events, shards, table_rows, data_size, loop_size, capacity):
    row_count, model_width = grad_events.shape
    slot_count = data_size * loop_size * capacity
    earlier = jnp.arange(row_count)[None, :] < jnp.arange(row_count)[:, None]
    matches = (shards[:, None] == shards[None, :]) & earlier
    slot_rank = jnp.sum(matches.astype(jnp.int32), axis=1)
    target = shards * capacity + slot_rank
    onehot = jnp.arange(slot_count, dtype=jnp.int32)[:, None] == target[None, :]
    packed = jnp.dot(
        onehot.astype(jnp.float32),
        grad_events,
        precision=lax.Precision.HIGHEST,
        preferred_element_type=jnp.float32,
    )
    labels = jnp.sum(jnp.where(onehot, table_rows[None, :] + 1, 0), axis=1) - 1
    return (
        packed.reshape(data_size, loop_size, capacity, model_width),
        labels.reshape(data_size, loop_size, capacity),
    )


def merge_rows(received, row_marks):
    model_width = received.shape[-1]
    flat_rows = received.reshape(-1, model_width)
    flat_marks = row_marks.reshape(-1)
    matches = ((flat_marks[:, None] == flat_marks[None, :]) & (flat_marks[None, :] >= 0)).astype(
        jnp.float32
    )
    return jnp.dot(
        matches, flat_rows, precision=lax.Precision.HIGHEST, preferred_element_type=jnp.float32
    )


def body(
    events,
    out_grad,
    proj_weight,
    out_weight,
    lengths,
    tile_mask,
    quotient_shard,
    quotient_row,
    remainder_shard,
    remainder_row,
):
    row_count, model_width = events.shape
    loop_size = lax.axis_size("ctx")
    data_size = lax.axis_size("dp")
    loop_place = lax.axis_index("ctx")
    longest = float(row_count * loop_size // 2)
    score_scale = 1.0 / math.sqrt(model_width // HEADS)
    history = lengths[0]
    row_start = loop_place * row_count
    projected = jnp.dot(events, proj_weight, preferred_element_type=jnp.float32)
    sigmoid_proj = jax.nn.sigmoid(projected)
    activated = (projected * sigmoid_proj).astype(jnp.bfloat16)
    gate_rows = activated[:, :model_width].astype(jnp.float32)
    value_rows = activated[:, model_width : 2 * model_width]
    query_rows = activated[:, 2 * model_width : 3 * model_width]
    key_rows = activated[:, 3 * model_width :]
    query_heads = query_rows.reshape(row_count, HEADS, -1)
    empty_rows = jnp.zeros((row_count, model_width), jnp.float32)

    def forward_turn(turn_index, state):
        running, key_block, value_block = state
        offset_row = (loop_place - turn_index) % loop_size * row_count
        weight = visible_weight(
            history, tile_mask, row_start, row_count, offset_row, row_count, longest
        )
        running = running + guarded(
            weight,
            lambda: forward_block(query_heads, key_block, value_block, weight, score_scale),
            empty_rows,
        )
        key_next, value_next = passed_along((key_block, value_block), "ctx", 1)
        return (running, key_next, value_next)

    mixed_rows, key_spent, value_spent = lax.fori_loop(
        0, loop_size, forward_turn, (empty_rows, key_rows, value_rows)
    )
    row_mean = jnp.mean(mixed_rows, axis=1, keepdims=True)
    centered = mixed_rows - row_mean
    inv_scale = lax.rsqrt(jnp.mean(centered * centered, axis=1, keepdims=True) + EPSILON)
    normed = centered * inv_scale
    gated_rows = (normed * gate_rows).astype(jnp.bfloat16)
    out_weight_term = jnp.einsum(
        "td,te->de", gated_rows, out_grad, preferred_element_type=jnp.float32
    )
    grad_gated = jnp.einsum("te,de->td", out_grad, out_weight, preferred_element_type=jnp.float32)
    grad_normed = grad_gated * gate_rows
    grad_gate = grad_gated * normed
    grad_mixed = (
        inv_scale
        * (
            grad_normed
            - jnp.mean(grad_normed, axis=1, keepdims=True)
            - normed * jnp.mean(grad_normed * normed, axis=1, keepdims=True)
        )
    ).astype(jnp.bfloat16)
    grad_heads = grad_mixed.reshape(row_count, HEADS, -1)
    empty_triple = (empty_rows, empty_rows, empty_rows)

    def cycle_turn(turn_index, state):
        grad_query, key_block, value_block, key_grad_block, value_grad_block = state
        offset_row = (loop_place - turn_index) % loop_size * row_count
        weight = visible_weight(
            history, tile_mask, row_start, row_count, offset_row, row_count, longest
        )
        query_add, key_add, value_add = guarded(
            weight,
            lambda: backward_block(
                query_heads, grad_heads, key_block, value_block, weight, score_scale
            ),
            empty_triple,
        )
        key_next, value_next = passed_along((key_block, value_block), "ctx", 1)
        key_grad_next, value_grad_next = from_behind(
            (key_grad_block + key_add, value_grad_block + value_add), "ctx", 1
        )
        return (grad_query + query_add, key_next, value_next, key_grad_next, value_grad_next)

    grad_query, key_back, value_back, grad_keys, grad_values = lax.fori_loop(
        0, loop_size, cycle_turn, (empty_rows, key_rows, value_rows, empty_rows, empty_rows)
    )
    grad_projected = (
        jnp.concatenate([grad_gate, grad_values, grad_query, grad_keys], axis=1)
        * silu_grad(projected, sigmoid_proj)
    ).astype(jnp.bfloat16)
    grad_events = out_grad.astype(jnp.float32) + jnp.einsum(
        "tf,df->td", grad_projected, proj_weight, preferred_element_type=jnp.float32
    )
    proj_weight_term = jnp.einsum(
        "td,tf->df", events, grad_projected, preferred_element_type=jnp.float32
    )
    proj_weight_grad, out_weight_grad = lax.psum((proj_weight_term, out_weight_term), ("dp", "ctx"))
    devices = data_size * loop_size
    capacity = max(2, 3 * row_count // (2 * devices))
    quotient_buffer, quotient_labels = pack_rows(
        grad_events, quotient_shard, quotient_row, data_size, loop_size, capacity
    )
    remainder_buffer, remainder_labels = pack_rows(
        grad_events, remainder_shard, remainder_row, data_size, loop_size, capacity
    )
    quotient_in, remainder_in, quotient_marks, remainder_marks = (
        lax.all_to_all(
            lax.all_to_all(quotient_buffer, "dp", split_axis=0, concat_axis=0, tiled=True),
            "ctx",
            split_axis=1,
            concat_axis=1,
            tiled=True,
        ),
        lax.all_to_all(
            lax.all_to_all(remainder_buffer, "dp", split_axis=0, concat_axis=0, tiled=True),
            "ctx",
            split_axis=1,
            concat_axis=1,
            tiled=True,
        ),
        lax.all_to_all(
            lax.all_to_all(quotient_labels, "dp", split_axis=0, concat_axis=0, tiled=True),
            "ctx",
            split_axis=1,
            concat_axis=1,
            tiled=True,
        ),
        lax.all_to_all(
            lax.all_to_all(remainder_labels, "dp", split_axis=0, concat_axis=0, tiled=True),
            "ctx",
            split_axis=1,
            concat_axis=1,
            tiled=True,
        ),
    )
    quotient_grads = merge_rows(quotient_in, quotient_marks)
    remainder_grads = merge_rows(remainder_in, remainder_marks)
    return (quotient_grads, remainder_grads, proj_weight_grad, out_weight_grad)


F32 = jnp.float32
BF16 = jnp.bfloat16
MESH = pl.DeviceIdType.MESH
BLOCK = 32
WIDTH = 512


def dot_rows(a, b):
    return lax.dot_general(a, b, (((1,), (1,)), ((), ())), preferred_element_type=F32)


def dot_first(a, b):
    return lax.dot_general(a, b, (((0,), (0,)), ((), ())), preferred_element_type=F32)


def sigmoid_of(x):
    return 0.5 * jnp.tanh(0.5 * x) + 0.5


def layer_kernel(
    data_size, lengths_ref, tiles_ref, ev_own, og_own, weight_ref, out_weight_ref,
    shards_ref, rows_ref, quotient_ref, remainder_ref, sum_ref,
    ev, og, act, dact, att, slope, mixed, gm, mask, gp, gated, pack, got_ref, chosen_slots, slot_numbers,
    part_a, part_b, part_c, income_a, income_b, income_c, outgo_a, outgo_b, outgo_c,
    totals_a, totals_b, totals_c,
    local_sem, ctx_send, ctx_recv, row_send, row_recv, red_send, red_recv, all_send, all_recv,
):
    half, width = ev_own.shape
    full = 2 * half
    data = lax.axis_index("dp")
    place = lax.axis_index("ctx")
    me = data * 2 + place
    devices = data_size * 2
    own = pl.multiple_of(place * half, half)
    far = pl.multiple_of((1 - place) * half, half)
    mine = pl.ds(own, half)
    across_x = (data, 1 - place)
    barrier = pltpu.get_barrier_semaphore()

    def other(k):
        to = lax.rem(me + k, devices)
        return to, (to // 2, lax.rem(to, 2))

    def remote(src, dst, send, recv, where):
        return pltpu.make_async_remote_copy(
            src_ref=src, dst_ref=dst, send_sem=send, recv_sem=recv, device_id=where,
            device_id_type=MESH,
        )

    @pl.loop(1, devices)
    def _(k):
        _, where = other(k)
        pl.semaphore_signal(barrier, inc=1, device_id=where, device_id_type=MESH)

    pl.semaphore_wait(barrier, devices - 1)
    ev_copy = remote(ev_own, ev.at[mine], ctx_send.at[0], ctx_recv.at[0], across_x)
    og_copy = remote(og_own, og.at[mine], ctx_send.at[1], ctx_recv.at[1], across_x)
    ev_copy.start()
    og_copy.start()
    ev[mine, :] = ev_own[...]
    og[mine, :] = og_own[...]

    def project(start):
        rows = pl.ds(start, half)

        @pl.loop(0, 4 * width // 256)
        def _(n):
            cols = pl.ds(pl.multiple_of(n * 256, 256), 256)
            projected = jnp.dot(ev[rows, :], weight_ref[:, cols], preferred_element_type=F32)
            sig = sigmoid_of(projected)
            act[rows, cols] = (projected * sig).astype(BF16)
            dact[rows, cols] = sig * (1.0 + projected * (1.0 - sig))

    project(own)

    ends = []
    total = jnp.int32(0)
    for k in range(lengths_ref.shape[1]):
        total = total + lengths_ref[0, k]
        ends.append(total)
    longest = float(full // 2)
    tiles = full // TILE
    mask[...] = jnp.zeros_like(mask)
    for a in range(tiles):
        row = a * TILE + lax.broadcasted_iota(jnp.int32, (TILE, TILE), 0)
        row_doc = sum((row >= e).astype(jnp.int32) for e in ends)
        for b in range(a + 1):
            col = b * TILE + lax.broadcasted_iota(jnp.int32, (TILE, TILE), 1)
            col_doc = sum((col >= e).astype(jnp.int32) for e in ends)
            keep = tiles_ref[a, b].astype(F32) / longest
            seen = (row_doc == col_doc) & (col <= row)
            mask[a * TILE : (a + 1) * TILE, b * TILE : (b + 1) * TILE] = jnp.where(seen, keep, 0.0)

    slots = pack.shape[0]
    capacity = 3 * half // (2 * (slots // BLOCK))
    early = lax.broadcasted_iota(jnp.int32, (half, half), 0) < lax.broadcasted_iota(
        jnp.int32, (half, half), 1
    )
    slot = lax.broadcasted_iota(jnp.int32, (slots, half), 0)
    spot = lax.broadcasted_iota(jnp.int32, (128, half), 0)
    onehot = jnp.zeros((slots, half), F32)
    numbers = jnp.zeros((slots, 128), F32)
    for t in range(2):
        shard = shards_ref[t : t + 1, :]
        across = jnp.broadcast_to(shard.astype(F32), (half, half))
        same = (jnp.transpose(across) == across) & early
        rank = jnp.sum(same.astype(F32), axis=0, keepdims=True).astype(jnp.int32)
        at = rank + t * capacity
        onehot = onehot + (slot == shard * BLOCK + at).astype(F32)
        number = rows_ref[t : t + 1, :]
        high = (number // 256 + 1).astype(F32)
        low = (number % 256).astype(F32)
        left = jnp.where(slot == shard * BLOCK + 2 * capacity, high, 0.0) + jnp.where(
            slot == shard * BLOCK + 2 * capacity + 1, low, 0.0
        )
        numbers = numbers + dot_rows(left.astype(BF16), (spot == at).astype(BF16))
    chosen_slots[...] = onehot.astype(BF16)
    slot_numbers[...] = numbers
    ev_copy.wait_recv()
    project(far)

    scale = 1.0 / math.sqrt(width // HEADS)
    head_width = width // HEADS
    lane = lax.broadcasted_iota(jnp.int32, (1, 128), 1) // head_width

    def pair_cols(base, p):
        return pl.ds(pl.multiple_of(base * width + p * 128, 128), 128)

    def only(x, h):
        return jnp.where(lane == h, x, jnp.zeros_like(x))

    blocks = ((0, half), (half, full))

    @pl.loop(0, width // 128)
    def _(p):
        q = (act[:, pair_cols(2, p)].astype(F32) * scale).astype(BF16)
        k = act[:, pair_cols(3, p)]
        v = act[:, pair_cols(1, p)]
        for lo, hi in blocks:
            total = jnp.zeros((half, 128), F32)
            for h in range(2):
                scores = dot_rows(only(q[lo:hi], h), k[:hi])
                sig = sigmoid_of(scores)
                w = mask[lo:hi, :hi]
                a = (scores * sig * w).astype(BF16)
                att[p * 2 + h, lo:hi, :hi] = a
                slope[p * 2 + h, lo:hi, :hi] = w * sig * (1.0 + scores * (1.0 - sig))
                total = total + jnp.dot(a, only(v[:hi], h), preferred_element_type=F32)
            mixed[lo:hi, pl.ds(pl.multiple_of(p * 128, 128), 128)] = total

    og_copy.wait_recv()

    @pl.loop(0, full // 128)
    def _(r):
        rows = pl.ds(pl.multiple_of(r * 128, 128), 128)
        m = mixed[rows, :]
        centered = m - jnp.mean(m, axis=1, keepdims=True)
        inv = lax.rsqrt(jnp.mean(centered * centered, axis=1, keepdims=True) + EPSILON)
        normed = centered * inv
        gate = act[rows, :width].astype(F32)
        gated[rows, :] = (normed * gate).astype(BF16)
        grad_gated = dot_rows(og[rows, :], out_weight_ref[...])
        grad_normed = grad_gated * gate
        gp[rows, :width] = (grad_gated * normed * dact[rows, :width]).astype(BF16)
        gm[rows, :] = (
            inv
            * (
                grad_normed
                - jnp.mean(grad_normed, axis=1, keepdims=True)
                - normed * jnp.mean(grad_normed * normed, axis=1, keepdims=True)
            )
        ).astype(BF16)

    def back_pair(p):
        q = (act[:, pair_cols(2, p)].astype(F32) * scale).astype(BF16)
        k = act[:, pair_cols(3, p)]
        v = act[:, pair_cols(1, p)]
        g = gm[:, pair_cols(0, p)]
        dv = [jnp.zeros((half, 128), F32)] * 2
        dk = [jnp.zeros((half, 128), F32)] * 2
        dq = [jnp.zeros((half, 128), F32)] * 2
        for h in range(2):
            kh, gh, qh = only(k, h), only(g, h), only(q, h)
            for n, (lo, hi) in enumerate(blocks):
                grad_att = dot_rows(gh[lo:hi], v[:hi])
                gs = (grad_att * slope[p * 2 + h, lo:hi, :hi]).astype(BF16)
                dq[n] = dq[n] + jnp.dot(gs, kh[:hi], preferred_element_type=F32)
                a = att[p * 2 + h, lo:hi, :hi]
                for m in range(n + 1):
                    at = slice(m * half, (m + 1) * half)
                    dv[m] = dv[m] + dot_first(a[:, at], gh[lo:hi])
                    dk[m] = dk[m] + dot_first(gs[:, at], qh[lo:hi])
        for n, (lo, hi) in enumerate(blocks):
            for base, value in ((1, dv[n]), (2, dq[n] * scale), (3, dk[n])):
                cols = pair_cols(base, p)
                gp[lo:hi, cols] = (value * dact[lo:hi, cols]).astype(BF16)

    def bit(n):
        return lax.rem(data // (1 << n), 2)

    def toward(n):
        return (data + (1 - 2 * bit(n)) * (1 << n), place)

    height = half
    layers = data_size // 4

    def travel(which, part, income, outgo, totals, left, last):
        wide = part.shape[1]
        columns = pl.ds(left, wide)

        def halving(n):
            size = height >> (n + 1)
            if n == 0:
                src = part.at[pl.ds(pl.multiple_of((1 - bit(0)) * size, size), size)]
            else:
                src = outgo.at[pl.ds(height - 2 * size, size)]
            dst = income.at[pl.ds(height - 2 * size, size)]
            return remote(src, dst, red_send.at[which, n], red_recv.at[which, n], toward(n))

        sent = [halving(0)]
        sent[0].start()
        yield
        offset = place * height
        for n in range(2):
            size = height >> (n + 1)
            came = pl.ds(height - 2 * size, size)
            sent[n].wait_recv()
            kept = pl.ds(pl.multiple_of(bit(n) * size, size), size)
            held = part[kept, :].astype(F32) if n == 0 else totals[kept, :]
            held = held + income[came, :].astype(F32)
            offset = offset + bit(n) * size
            totals[:size, :] = held
            if n == 0:
                small = size // 2
                gone = pl.ds(pl.multiple_of((1 - bit(1)) * small, small), small)
                outgo[pl.ds(height - 2 * small, small), :] = totals[gone, :].astype(BF16)
                sent.append(halving(1))
                sent[1].start()
                yield
        size = height // data_size
        low = height - height // 4
        outgo[pl.ds(low, layers * size), :] = totals[: layers * size, :].astype(BF16)
        layer = data // 4
        for k in range(1, layers):
            to = lax.rem(layer + k, layers)
            src = outgo.at[pl.ds(pl.multiple_of(low + to * size, size), size)]
            dst = income.at[pl.ds(low + (k - 1) * size, size)]
            copy = remote(
                src, dst, red_send.at[which, 1 + k], red_recv.at[which, 1 + k],
                (to * 4 + lax.rem(data, 4), place),
            )
            copy.start()
            sent.append(copy)
        yield
        held = totals[pl.ds(pl.multiple_of(layer * size, size), size), :]
        for k in range(1, layers):
            sent[1 + k].wait_recv()
            held = held + income[pl.ds(low + (k - 1) * size, size), :].astype(F32)
        region = offset
        offset = offset + layer * size
        sum_ref[pl.ds(pl.multiple_of(offset, size), size), columns] = held.astype(BF16)

        count = [0]

        def spread(start, size, where):
            rows = sum_ref.at[pl.ds(pl.multiple_of(start, 16), size), columns]
            n = count[0]
            count[0] += 1
            copy = remote(rows, rows, all_send.at[which, n], all_recv.at[which, n], where)
            copy.start()
            sent.append(copy)
            return copy

        copies = [
            spread(offset, size, (lax.rem(layer + k, layers) * 4 + lax.rem(data, 4), place))
            for k in range(1, layers)
        ]
        yield
        for copy in copies:
            copy.wait_recv()
        offset = region
        size = layers * size
        mirror = (1 - 2 * place) * height
        if last == "x":
            copy = spread(offset, size, toward(1))
            yield
            copy.wait_recv()
            offset = offset - bit(1) * size
            size = 2 * size
            first = spread(offset, size, across_x)
            near = spread(offset, size, toward(0))
            yield
            first.wait_recv()
            back = spread(offset + mirror, size, toward(0))
            yield
            near.wait_recv()
            back.wait_recv()
        else:
            first = spread(offset, size, across_x)
            second = spread(offset, size, toward(1))
            yield
            first.wait_recv()
            third = spread(offset + mirror, size, toward(1))
            yield
            second.wait_recv()
            offset = offset - bit(1) * size
            size = 2 * size
            near = spread(offset, size, toward(0))
            third.wait_recv()
            back = spread(offset + mirror, size, toward(0))
            yield
            near.wait_recv()
            back.wait_recv()
        for copy in sent:
            copy.wait_send()

    part_a[:, :width] = dot_first(gated[:, mine], og[...]).astype(BF16)
    ev_mine = ev[:, mine]
    part_a[:, width:] = dot_first(ev_mine, gp[:, :width]).astype(BF16)
    run_a = travel(0, part_a, income_a, outgo_a, totals_a, 0, "x")
    next(run_a)

    pairs = width // 128
    piece = width // 2

    def late(part, which):
        for n in range(3):
            cols = slice((n + 1) * width + which * piece, (n + 1) * width + (which + 1) * piece)
            part[:, n * piece : (n + 1) * piece] = dot_first(ev_mine, gp[:, cols]).astype(BF16)

    pl.loop(0, pairs // 2)(back_pair)
    next(run_a)
    late(part_b, 0)
    run_b = travel(1, part_b, income_b, outgo_b, totals_b, 2 * width, "y")
    next(run_b)
    pl.loop(pairs // 2, pairs)(back_pair)
    next(run_a)
    next(run_b)
    late(part_c, 1)
    run_c = travel(2, part_c, income_c, outgo_c, totals_c, 2 * width + 3 * piece, "y")
    next(run_c)
    next(run_a)
    next(run_b)

    grad_events = (og_own[...].astype(F32) + dot_rows(gp[mine, :], weight_ref[...])).astype(BF16)
    packed = jnp.dot(chosen_slots[...], grad_events, preferred_element_type=F32)
    pack[:, :128] = (packed[:, :128] + slot_numbers[...]).astype(BF16)
    pack[:, 128:] = packed[:, 128:].astype(BF16)

    def row_copy(k):
        to, where = other(k)
        return remote(
            pack.at[pl.ds(pl.multiple_of(to * BLOCK, BLOCK), BLOCK)],
            got_ref.at[pl.ds(pl.multiple_of(me * BLOCK, BLOCK), BLOCK)],
            row_send.at[k],
            row_recv.at[k],
            where,
        )

    here = pl.ds(pl.multiple_of(me * BLOCK, BLOCK), BLOCK)
    local = pltpu.make_async_copy(pack.at[here], got_ref.at[here], local_sem)
    local.start()

    fourth = devices // 4
    turns = [[k for k in (g + fourth, g + 2 * fourth, g + 3 * fourth, g) if k] for g in range(fourth)]
    running = [run_a, run_b, run_c]
    for count in (2, 2, 2, 1, 1, 0):
        for _ in range(count):
            for k in turns.pop(0):
                row_copy(k).start()
        running = [run for run in running if next(run, "end") != "end"]

    local.wait()

    @pl.loop(1, devices)
    def _(k):
        row_copy(k).wait_recv()

    side = lax.broadcasted_iota(jnp.int32, (devices, slots), 0)
    flat = lax.broadcasted_iota(jnp.int32, (devices, slots), 1)
    found = []
    for n in range(2):
        pick = (flat == side * BLOCK + 2 * capacity + n).astype(BF16)
        found.append(
            jnp.dot(pick, got_ref[:, :128], preferred_element_type=F32).astype(BF16)
        )

    def keys_of(count, block, first):
        row = lax.broadcasted_iota(jnp.int32, (count, devices), 0) // block
        of = (row == lax.broadcasted_iota(jnp.int32, (count, devices), 1)).astype(BF16)
        high = jnp.dot(of, found[0], preferred_element_type=F32)
        low = jnp.dot(of, found[1], preferred_element_type=F32)
        spot_row = lax.broadcasted_iota(jnp.int32, (count, 128), 0) % block + first
        spot_lane = lax.broadcasted_iota(jnp.int32, (count, 128), 1)
        key = jnp.where((spot_row == spot_lane) & (spot_lane < 2 * capacity), high * 256.0 + low, 0.0)
        return jnp.sum(key, axis=1, keepdims=True)

    column = jnp.broadcast_to(keys_of(slots, BLOCK, 0), (slots, 128))
    line = jnp.transpose(column)[0:1, :]
    spot_line = lax.broadcasted_iota(jnp.int32, (1, slots), 1) % BLOCK
    for t, out in enumerate((quotient_ref, remainder_ref)):
        wanted = keys_of(out.shape[0], capacity, t * capacity)
        inside = (spot_line >= t * capacity) & (spot_line < (t + 1) * capacity) & (line > 0.0)
        match = ((wanted == line) & inside).astype(BF16)
        out[...] = jnp.dot(match, got_ref[...], preferred_element_type=F32)

    while running:
        running = [run for run in running if next(run, "end") != "end"]

    ev_copy.wait_send()
    og_copy.wait_send()

    @pl.loop(1, devices)
    def _(k):
        row_copy(k).wait_send()


def pair_body(
    events, out_grad, proj_weight, out_weight, lengths, tile_mask,
    quotient_shard, quotient_row, remainder_shard, remainder_row,
):
    half, width = events.shape
    data_size = lax.axis_size("dp")
    devices = 2 * data_size
    capacity = 3 * half // (2 * devices)
    full = 2 * half
    shards = jnp.stack([quotient_shard, remainder_shard])
    numbers = jnp.stack([quotient_row, remainder_row])
    vmem = pl.BlockSpec(memory_space=pltpu.VMEM)
    smem = pl.BlockSpec(memory_space=pltpu.SMEM)
    layers = data_size // 4
    wides = (2 * width, 3 * width // 2, 3 * width // 2)
    quotient, remainder, sums = pl.pallas_call(
        lambda *refs: layer_kernel(data_size, *refs),
        name="layer",
        out_shape=(
            jax.ShapeDtypeStruct((devices * capacity, width), F32),
            jax.ShapeDtypeStruct((devices * capacity, width), F32),
            jax.ShapeDtypeStruct((full, 5 * width), BF16),
        ),
        in_specs=[smem] * 2 + [vmem] * 6,
        out_specs=(vmem, vmem, vmem),
        scratch_shapes=[
            pltpu.VMEM((full, width), BF16),
            pltpu.VMEM((full, width), BF16),
            pltpu.VMEM((full, 4 * width), BF16),
            pltpu.VMEM((full, 4 * width), F32),
            pltpu.VMEM((HEADS, full, full), BF16),
            pltpu.VMEM((HEADS, full, full), F32),
            pltpu.VMEM((full, width), F32),
            pltpu.VMEM((full, width), BF16),
            pltpu.VMEM((full, full), F32),
            pltpu.VMEM((full, 4 * width), BF16),
            pltpu.VMEM((full, width), BF16),
            pltpu.VMEM((devices * BLOCK, width), BF16),
            pltpu.VMEM((devices * BLOCK, width), BF16),
            pltpu.VMEM((devices * BLOCK, half), BF16),
            pltpu.VMEM((devices * BLOCK, 128), F32),
            *[pltpu.VMEM((half, wide), BF16) for wide in wides],
            *[pltpu.VMEM((half, wide), BF16) for wide in wides],
            *[pltpu.VMEM((half, wide), BF16) for wide in wides],
            *[pltpu.VMEM((half // 2, wide), F32) for wide in wides],
            pltpu.SemaphoreType.DMA,
            pltpu.SemaphoreType.DMA((2,)),
            pltpu.SemaphoreType.DMA((2,)),
            pltpu.SemaphoreType.DMA((devices,)),
            pltpu.SemaphoreType.DMA((devices,)),
            pltpu.SemaphoreType.DMA((3, layers + 1)),
            pltpu.SemaphoreType.DMA((3, layers + 1)),
            pltpu.SemaphoreType.DMA((3, layers + 4)),
            pltpu.SemaphoreType.DMA((3, layers + 4)),
        ],
        compiler_params=pltpu.CompilerParams(
            collective_id=0, has_side_effects=True, vmem_limit_bytes=56 * 2**20
        ),
        cost_estimate=pl.CostEstimate(
            flops=10 * 10**9, bytes_accessed=8 * 2**20, transcendentals=4 * 10**6
        ),
    )(
        lengths, tile_mask, events, out_grad, proj_weight, out_weight, shards, numbers,
    )
    piece = width // 2
    proj_grad = [sums[:, 2 * piece : 4 * piece]]
    for n in range(3):
        for h in range(2):
            start = (4 + 3 * h + n) * piece
            proj_grad.append(sums[:, start : start + piece])
    return (
        quotient,
        remainder,
        jnp.concatenate(proj_grad, axis=1).astype(F32),
        sums[:, :width].astype(F32),
    )


def pair_fits(mesh):
    data_size, loop_size = mesh.shape["dp"], mesh.shape["ctx"]
    return loop_size == 2 and data_size == 16


def solution(mesh):
    chosen = pair_body if pair_fits(mesh) else body
    in_specs = (
        P(("dp", "ctx"), None),
        P(("dp", "ctx"), None),
        P(),
        P(),
        P("dp", None),
        P("dp", None),
        P(("dp", "ctx")),
        P(("dp", "ctx")),
        P(("dp", "ctx")),
        P(("dp", "ctx")),
    )
    out_specs = (P(("dp", "ctx"), None), P(("dp", "ctx"), None), P(), P())
    return jax.shard_map(chosen, mesh=mesh, in_specs=in_specs, out_specs=out_specs, check_vma=False)
```

```python
import math

import jax
import jax.numpy as jnp
from jax import lax
from jax.experimental import pallas as pl
from jax.experimental.pallas import tpu as pltpu
from jax.sharding import PartitionSpec as P

HEADS = 8
TILE = 128


EPSILON = 1e-05


def passed_along(shard, axis, by):
    count = lax.axis_size(axis)
    pairs = [(i, i + by) for i in range(count) if 0 <= i + by < count]
    return lax.ppermute(shard, axis, pairs)


def from_behind(shard, axis, by):
    count = lax.axis_size(axis)
    return lax.ppermute(shard, axis, [(i, (i + by) % count) for i in range(count)])


def silu_grad(value, sigma):
    return sigma * (1.0 + value * (1.0 - sigma))


def visible_weight(history, tile_table, row_start, row_count, col_start, col_count, longest):
    row_pos = row_start + jnp.arange(row_count, dtype=jnp.int32)
    col_pos = col_start + jnp.arange(col_count, dtype=jnp.int32)
    doc_ends = jnp.cumsum(history)
    row_doc = jnp.sum((row_pos[:, None] >= doc_ends[None, :]).astype(jnp.int32), axis=1)
    col_doc = jnp.sum((col_pos[:, None] >= doc_ends[None, :]).astype(jnp.int32), axis=1)
    tile_ids = jnp.arange(tile_table.shape[0], dtype=jnp.int32)
    row_tiles = (row_pos[:, None] // TILE == tile_ids[None, :]).astype(jnp.float32)
    col_tiles = (col_pos[:, None] // TILE == tile_ids[None, :]).astype(jnp.float32)
    tile_rows = jnp.dot(row_tiles, tile_table.astype(jnp.float32), precision=lax.Precision.HIGHEST)
    tile_full = jnp.dot(tile_rows, col_tiles.T, precision=lax.Precision.HIGHEST)
    visible = (
        (row_doc[:, None] == col_doc[None, :])
        & (col_pos[None, :] <= row_pos[:, None])
        & (tile_full > 0.5)
    )
    return visible.astype(jnp.float32) / longest


def guarded(weight, compute, empty_result):
    return lax.cond(jnp.any(weight > 0.0), compute, lambda: empty_result)


def forward_block(query_heads, key_rows, value_rows, weight, score_scale):
    col_count = key_rows.shape[0]
    key_heads = key_rows.reshape(col_count, HEADS, -1)
    value_heads = value_rows.reshape(col_count, HEADS, -1)
    scores = (
        jnp.einsum("ihd,jhd->hij", query_heads, key_heads, preferred_element_type=jnp.float32)
        * score_scale
    )
    attention = (scores * jax.nn.sigmoid(scores) * weight[None]).astype(jnp.bfloat16)
    mixed_rows = jnp.einsum(
        "hij,jhd->ihd", attention, value_heads, preferred_element_type=jnp.float32
    )
    return mixed_rows.reshape(query_heads.shape[0], -1)


def backward_block(query_heads, grad_heads, key_rows, value_rows, weight, score_scale):
    col_count = key_rows.shape[0]
    row_count = query_heads.shape[0]
    key_heads = key_rows.reshape(col_count, HEADS, -1)
    value_heads = value_rows.reshape(col_count, HEADS, -1)
    scores = (
        jnp.einsum("ihd,jhd->hij", query_heads, key_heads, preferred_element_type=jnp.float32)
        * score_scale
    )
    sigmoid_scores = jax.nn.sigmoid(scores)
    attention = (scores * sigmoid_scores * weight[None]).astype(jnp.bfloat16)
    grad_attention = jnp.einsum(
        "ihd,jhd->hij", grad_heads, value_heads, preferred_element_type=jnp.float32
    )
    grad_scores = (grad_attention * weight[None] * silu_grad(scores, sigmoid_scores)).astype(
        jnp.bfloat16
    )
    grad_values = jnp.einsum(
        "hij,ihd->jhd", attention, grad_heads, preferred_element_type=jnp.float32
    ).reshape(col_count, -1)
    grad_query = (
        jnp.einsum(
            "hij,jhd->ihd", grad_scores, key_heads, preferred_element_type=jnp.float32
        ).reshape(row_count, -1)
        * score_scale
    )
    grad_keys = (
        jnp.einsum(
            "hij,ihd->jhd", grad_scores, query_heads, preferred_element_type=jnp.float32
        ).reshape(col_count, -1)
        * score_scale
    )
    return (grad_query, grad_keys, grad_values)


def pack_rows(grad_events, shards, table_rows, data_size, loop_size, capacity):
    row_count, model_width = grad_events.shape
    slot_count = data_size * loop_size * capacity
    earlier = jnp.arange(row_count)[None, :] < jnp.arange(row_count)[:, None]
    matches = (shards[:, None] == shards[None, :]) & earlier
    slot_rank = jnp.sum(matches.astype(jnp.int32), axis=1)
    target = shards * capacity + slot_rank
    onehot = jnp.arange(slot_count, dtype=jnp.int32)[:, None] == target[None, :]
    packed = jnp.dot(
        onehot.astype(jnp.float32),
        grad_events,
        precision=lax.Precision.HIGHEST,
        preferred_element_type=jnp.float32,
    )
    labels = jnp.sum(jnp.where(onehot, table_rows[None, :] + 1, 0), axis=1) - 1
    return (
        packed.reshape(data_size, loop_size, capacity, model_width),
        labels.reshape(data_size, loop_size, capacity),
    )


def merge_rows(received, row_marks):
    model_width = received.shape[-1]
    flat_rows = received.reshape(-1, model_width)
    flat_marks = row_marks.reshape(-1)
    matches = ((flat_marks[:, None] == flat_marks[None, :]) & (flat_marks[None, :] >= 0)).astype(
        jnp.float32
    )
    return jnp.dot(
        matches, flat_rows, precision=lax.Precision.HIGHEST, preferred_element_type=jnp.float32
    )


def body(
    events,
    out_grad,
    proj_weight,
    out_weight,
    lengths,
    tile_mask,
    quotient_shard,
    quotient_row,
    remainder_shard,
    remainder_row,
):
    row_count, model_width = events.shape
    loop_size = lax.axis_size("ctx")
    data_size = lax.axis_size("dp")
    loop_place = lax.axis_index("ctx")
    longest = float(row_count * loop_size // 2)
    score_scale = 1.0 / math.sqrt(model_width // HEADS)
    history = lengths[0]
    row_start = loop_place * row_count
    projected = jnp.dot(events, proj_weight, preferred_element_type=jnp.float32)
    sigmoid_proj = jax.nn.sigmoid(projected)
    activated = (projected * sigmoid_proj).astype(jnp.bfloat16)
    gate_rows = activated[:, :model_width].astype(jnp.float32)
    value_rows = activated[:, model_width : 2 * model_width]
    query_rows = activated[:, 2 * model_width : 3 * model_width]
    key_rows = activated[:, 3 * model_width :]
    query_heads = query_rows.reshape(row_count, HEADS, -1)
    empty_rows = jnp.zeros((row_count, model_width), jnp.float32)

    def forward_turn(turn_index, state):
        running, key_block, value_block = state
        offset_row = (loop_place - turn_index) % loop_size * row_count
        weight = visible_weight(
            history, tile_mask, row_start, row_count, offset_row, row_count, longest
        )
        running = running + guarded(
            weight,
            lambda: forward_block(query_heads, key_block, value_block, weight, score_scale),
            empty_rows,
        )
        key_next, value_next = passed_along((key_block, value_block), "ctx", 1)
        return (running, key_next, value_next)

    mixed_rows, key_spent, value_spent = lax.fori_loop(
        0, loop_size, forward_turn, (empty_rows, key_rows, value_rows)
    )
    row_mean = jnp.mean(mixed_rows, axis=1, keepdims=True)
    centered = mixed_rows - row_mean
    inv_scale = lax.rsqrt(jnp.mean(centered * centered, axis=1, keepdims=True) + EPSILON)
    normed = centered * inv_scale
    gated_rows = (normed * gate_rows).astype(jnp.bfloat16)
    out_weight_term = jnp.einsum(
        "td,te->de", gated_rows, out_grad, preferred_element_type=jnp.float32
    )
    grad_gated = jnp.einsum("te,de->td", out_grad, out_weight, preferred_element_type=jnp.float32)
    grad_normed = grad_gated * gate_rows
    grad_gate = grad_gated * normed
    grad_mixed = (
        inv_scale
        * (
            grad_normed
            - jnp.mean(grad_normed, axis=1, keepdims=True)
            - normed * jnp.mean(grad_normed * normed, axis=1, keepdims=True)
        )
    ).astype(jnp.bfloat16)
    grad_heads = grad_mixed.reshape(row_count, HEADS, -1)
    empty_triple = (empty_rows, empty_rows, empty_rows)

    def cycle_turn(turn_index, state):
        grad_query, key_block, value_block, key_grad_block, value_grad_block = state
        offset_row = (loop_place - turn_index) % loop_size * row_count
        weight = visible_weight(
            history, tile_mask, row_start, row_count, offset_row, row_count, longest
        )
        query_add, key_add, value_add = guarded(
            weight,
            lambda: backward_block(
                query_heads, grad_heads, key_block, value_block, weight, score_scale
            ),
            empty_triple,
        )
        key_next, value_next = passed_along((key_block, value_block), "ctx", 1)
        key_grad_next, value_grad_next = from_behind(
            (key_grad_block + key_add, value_grad_block + value_add), "ctx", 1
        )
        return (grad_query + query_add, key_next, value_next, key_grad_next, value_grad_next)

    grad_query, key_back, value_back, grad_keys, grad_values = lax.fori_loop(
        0, loop_size, cycle_turn, (empty_rows, key_rows, value_rows, empty_rows, empty_rows)
    )
    grad_projected = (
        jnp.concatenate([grad_gate, grad_values, grad_query, grad_keys], axis=1)
        * silu_grad(projected, sigmoid_proj)
    ).astype(jnp.bfloat16)
    grad_events = out_grad.astype(jnp.float32) + jnp.einsum(
        "tf,df->td", grad_projected, proj_weight, preferred_element_type=jnp.float32
    )
    proj_weight_term = jnp.einsum(
        "td,tf->df", events, grad_projected, preferred_element_type=jnp.float32
    )
    proj_weight_grad, out_weight_grad = lax.psum((proj_weight_term, out_weight_term), ("dp", "ctx"))
    devices = data_size * loop_size
    capacity = max(2, 3 * row_count // (2 * devices))
    quotient_buffer, quotient_labels = pack_rows(
        grad_events, quotient_shard, quotient_row, data_size, loop_size, capacity
    )
    remainder_buffer, remainder_labels = pack_rows(
        grad_events, remainder_shard, remainder_row, data_size, loop_size, capacity
    )
    quotient_in, remainder_in, quotient_marks, remainder_marks = (
        lax.all_to_all(
            lax.all_to_all(quotient_buffer, "dp", split_axis=0, concat_axis=0, tiled=True),
            "ctx",
            split_axis=1,
            concat_axis=1,
            tiled=True,
        ),
        lax.all_to_all(
            lax.all_to_all(remainder_buffer, "dp", split_axis=0, concat_axis=0, tiled=True),
            "ctx",
            split_axis=1,
            concat_axis=1,
            tiled=True,
        ),
        lax.all_to_all(
            lax.all_to_all(quotient_labels, "dp", split_axis=0, concat_axis=0, tiled=True),
            "ctx",
            split_axis=1,
            concat_axis=1,
            tiled=True,
        ),
        lax.all_to_all(
            lax.all_to_all(remainder_labels, "dp", split_axis=0, concat_axis=0, tiled=True),
            "ctx",
            split_axis=1,
            concat_axis=1,
            tiled=True,
        ),
    )
    quotient_grads = merge_rows(quotient_in, quotient_marks)
    remainder_grads = merge_rows(remainder_in, remainder_marks)
    return (quotient_grads, remainder_grads, proj_weight_grad, out_weight_grad)


F32 = jnp.float32
BF16 = jnp.bfloat16
MESH = pl.DeviceIdType.MESH
MARK = 16


def dot_rows(a, b):
    return lax.dot_general(a, b, (((1,), (1,)), ((), ())), preferred_element_type=F32)


def dot_first(a, b):
    return lax.dot_general(a, b, (((0,), (0,)), ((), ())), preferred_element_type=F32)


def sigmoid_of(x):
    return 0.5 * jnp.tanh(0.5 * x) + 0.5


def layer_kernel(
    data_size, lengths_ref, tiles_ref, ev_own, og_own, weight_ref, out_weight_ref,
    info_ref, quotient_ref, remainder_ref, sum_ref,
    ev, og, act, dact, att, slope, mixed, gm, mask, gp, gated, pack, got_ref, info, chosen_slots, marks, marks_in,
    part_a, part_b, part_c, income_a, income_b, income_c, outgo_a, outgo_b, outgo_c,
    totals_a, totals_b, totals_c,
    local_sem, ctx_send, ctx_recv, row_send, row_recv, mark_send, mark_recv, red_send, red_recv, all_send, all_recv,
):
    half, width = ev_own.shape
    full = 2 * half
    data = lax.axis_index("dp")
    place = lax.axis_index("ctx")
    me = data * 2 + place
    devices = data_size * 2
    own = pl.multiple_of(place * half, half)
    far = pl.multiple_of((1 - place) * half, half)
    mine = pl.ds(own, half)
    across_x = (data, 1 - place)
    barrier = pltpu.get_barrier_semaphore()

    def other(k):
        to = lax.rem(data + k, data_size)
        return to, (to, place)

    def remote(src, dst, send, recv, where):
        return pltpu.make_async_remote_copy(
            src_ref=src, dst_ref=dst, send_sem=send, recv_sem=recv, device_id=where,
            device_id_type=MESH,
        )

    pl.semaphore_signal(barrier, inc=1, device_id=across_x, device_id_type=MESH)

    @pl.loop(1, data_size)
    def _(k):
        _, where = other(k)
        pl.semaphore_signal(barrier, inc=1, device_id=where, device_id_type=MESH)

    pl.semaphore_wait(barrier, data_size)
    my_info = pl.ds(pl.multiple_of(place * 8, 8), 8)
    info_copy = remote(info_ref, info.at[my_info], ctx_send.at[2], ctx_recv.at[2], across_x)
    info_copy.start()
    info[my_info, :] = info_ref[...]
    ev_copy = remote(ev_own, ev.at[mine], ctx_send.at[0], ctx_recv.at[0], across_x)
    og_copy = remote(og_own, og.at[mine], ctx_send.at[1], ctx_recv.at[1], across_x)
    ev_copy.start()
    og_copy.start()
    ev[mine, :] = ev_own[...]
    og[mine, :] = og_own[...]

    def project(start):
        rows = pl.ds(start, half)

        @pl.loop(0, 4 * width // 256)
        def _(n):
            cols = pl.ds(pl.multiple_of(n * 256, 256), 256)
            projected = jnp.dot(ev[rows, :], weight_ref[:, cols], preferred_element_type=F32)
            sig = sigmoid_of(projected)
            act[rows, cols] = (projected * sig).astype(BF16)
            dact[rows, cols] = sig * (1.0 + projected * (1.0 - sig))

    project(own)

    ends = []
    total = jnp.int32(0)
    for k in range(lengths_ref.shape[1]):
        total = total + lengths_ref[0, k]
        ends.append(total)
    longest = float(full // 2)
    tiles = full // TILE
    mask[...] = jnp.zeros_like(mask)
    for a in range(tiles):
        row = a * TILE + lax.broadcasted_iota(jnp.int32, (TILE, TILE), 0)
        row_doc = sum((row >= e).astype(jnp.int32) for e in ends)
        for b in range(a + 1):
            col = b * TILE + lax.broadcasted_iota(jnp.int32, (TILE, TILE), 1)
            col_doc = sum((col >= e).astype(jnp.int32) for e in ends)
            keep = tiles_ref[a, b].astype(F32) / longest
            seen = (row_doc == col_doc) & (col <= row)
            mask[a * TILE : (a + 1) * TILE, b * TILE : (b + 1) * TILE] = jnp.where(seen, keep, 0.0)

    info_copy.wait_recv()
    slots = pack.shape[0]
    capacity = 3 * half // (2 * devices)
    block = 4 * capacity
    early = lax.broadcasted_iota(jnp.int32, (half, half), 0) < lax.broadcasted_iota(
        jnp.int32, (half, half), 1
    )
    slot = lax.broadcasted_iota(jnp.int32, (slots, half), 0)
    mark_row = lax.broadcasted_iota(jnp.int32, (data_size * MARK, half), 0)
    spot = lax.broadcasted_iota(jnp.int32, (128, half), 0)
    numbers = jnp.zeros((data_size * MARK, 128), F32)
    for side in range(2):
        onehot = jnp.zeros((slots, half), F32)
        for t in range(2):
            shard = info[side * 8 + t : side * 8 + t + 1, :]
            across = jnp.broadcast_to(shard.astype(F32), (half, half))
            same = (jnp.transpose(across) == across) & early
            rank = jnp.sum(same.astype(F32), axis=0, keepdims=True).astype(jnp.int32)
            at = rank + (2 * side + t) * capacity
            owner = jnp.where(shard % 2 == place, shard // 2, -100)
            onehot = onehot + (slot == owner * block + at).astype(F32)
            number = info[side * 8 + 2 + t : side * 8 + 3 + t, :]
            high = (number // 256 + 1).astype(F32)
            low = (number % 256).astype(F32)
            left = jnp.where(mark_row == owner * MARK, high, 0.0) + jnp.where(
                mark_row == owner * MARK + 1, low, 0.0
            )
            numbers = numbers + dot_rows(left.astype(BF16), (spot == at).astype(BF16))
        chosen_slots[:, side * half : (side + 1) * half] = onehot.astype(BF16)
    marks[...] = numbers.astype(BF16)

    def block_copy(k, src, dst, size, send, recv):
        to, where = other(k)
        return remote(
            src.at[pl.ds(pl.multiple_of(to * size, size), size)],
            dst.at[pl.ds(pl.multiple_of(data * size, size), size)],
            send.at[k],
            recv.at[k],
            where,
        )

    def mark_copy(k):
        return block_copy(k, marks, marks_in, MARK, mark_send, mark_recv)

    def row_copy(k):
        return block_copy(k, pack, got_ref, block, row_send, row_recv)

    @pl.loop(1, data_size)
    def _(k):
        mark_copy(k).start()

    marks_here = pl.ds(pl.multiple_of(data * MARK, MARK), MARK)
    marks_in[marks_here, :] = marks[marks_here, :]

    ev_copy.wait_recv()
    project(far)

    scale = 1.0 / math.sqrt(width // HEADS)
    head_width = width // HEADS
    lane = lax.broadcasted_iota(jnp.int32, (1, 128), 1) // head_width

    def pair_cols(base, p):
        return pl.ds(pl.multiple_of(base * width + p * 128, 128), 128)

    def only(x, h):
        return jnp.where(lane == h, x, jnp.zeros_like(x))

    blocks = ((0, half), (half, full))

    @pl.loop(0, width // 128)
    def _(p):
        q = (act[:, pair_cols(2, p)].astype(F32) * scale).astype(BF16)
        k = act[:, pair_cols(3, p)]
        v = act[:, pair_cols(1, p)]
        for lo, hi in blocks:
            total = jnp.zeros((half, 128), F32)
            for h in range(2):
                scores = dot_rows(only(q[lo:hi], h), k[:hi])
                sig = sigmoid_of(scores)
                w = mask[lo:hi, :hi]
                a = (scores * sig * w).astype(BF16)
                att[p * 2 + h, lo:hi, :hi] = a
                slope[p * 2 + h, lo:hi, :hi] = w * sig * (1.0 + scores * (1.0 - sig))
                total = total + jnp.dot(a, only(v[:hi], h), preferred_element_type=F32)
            mixed[lo:hi, pl.ds(pl.multiple_of(p * 128, 128), 128)] = total

    og_copy.wait_recv()

    @pl.loop(0, full // 128)
    def _(r):
        rows = pl.ds(pl.multiple_of(r * 128, 128), 128)
        m = mixed[rows, :]
        centered = m - jnp.mean(m, axis=1, keepdims=True)
        inv = lax.rsqrt(jnp.mean(centered * centered, axis=1, keepdims=True) + EPSILON)
        normed = centered * inv
        gate = act[rows, :width].astype(F32)
        gated[rows, :] = (normed * gate).astype(BF16)
        grad_gated = dot_rows(og[rows, :], out_weight_ref[...])
        grad_normed = grad_gated * gate
        gp[rows, :width] = (grad_gated * normed * dact[rows, :width]).astype(BF16)
        gm[rows, :] = (
            inv
            * (
                grad_normed
                - jnp.mean(grad_normed, axis=1, keepdims=True)
                - normed * jnp.mean(grad_normed * normed, axis=1, keepdims=True)
            )
        ).astype(BF16)

    def back_pair(p):
        q = (act[:, pair_cols(2, p)].astype(F32) * scale).astype(BF16)
        k = act[:, pair_cols(3, p)]
        v = act[:, pair_cols(1, p)]
        g = gm[:, pair_cols(0, p)]
        dv = [jnp.zeros((half, 128), F32)] * 2
        dk = [jnp.zeros((half, 128), F32)] * 2
        dq = [jnp.zeros((half, 128), F32)] * 2
        for h in range(2):
            kh, gh, qh = only(k, h), only(g, h), only(q, h)
            for n, (lo, hi) in enumerate(blocks):
                grad_att = dot_rows(gh[lo:hi], v[:hi])
                gs = (grad_att * slope[p * 2 + h, lo:hi, :hi]).astype(BF16)
                dq[n] = dq[n] + jnp.dot(gs, kh[:hi], preferred_element_type=F32)
                a = att[p * 2 + h, lo:hi, :hi]
                for m in range(n + 1):
                    at = slice(m * half, (m + 1) * half)
                    dv[m] = dv[m] + dot_first(a[:, at], gh[lo:hi])
                    dk[m] = dk[m] + dot_first(gs[:, at], qh[lo:hi])
        for n, (lo, hi) in enumerate(blocks):
            for base, value in ((1, dv[n]), (2, dq[n] * scale), (3, dk[n])):
                cols = pair_cols(base, p)
                gp[lo:hi, cols] = (value * dact[lo:hi, cols]).astype(BF16)

    def bit(n):
        return lax.rem(data // (1 << n), 2)

    def toward(n):
        return (data + (1 - 2 * bit(n)) * (1 << n), place)

    height = half
    layers = data_size // 4

    def travel(which, part, income, outgo, totals, left, last):
        wide = part.shape[1]
        columns = pl.ds(left, wide)

        def halving(n):
            size = height >> (n + 1)
            if n == 0:
                src = part.at[pl.ds(pl.multiple_of((1 - bit(0)) * size, size), size)]
            else:
                src = outgo.at[pl.ds(height - 2 * size, size)]
            dst = income.at[pl.ds(height - 2 * size, size)]
            return remote(src, dst, red_send.at[which, n], red_recv.at[which, n], toward(n))

        sent = [halving(0)]
        sent[0].start()
        yield
        offset = place * height
        for n in range(2):
            size = height >> (n + 1)
            came = pl.ds(height - 2 * size, size)
            sent[n].wait_recv()
            kept = pl.ds(pl.multiple_of(bit(n) * size, size), size)
            held = part[kept, :].astype(F32) if n == 0 else totals[kept, :]
            held = held + income[came, :].astype(F32)
            offset = offset + bit(n) * size
            totals[:size, :] = held
            if n == 0:
                small = size // 2
                gone = pl.ds(pl.multiple_of((1 - bit(1)) * small, small), small)
                outgo[pl.ds(height - 2 * small, small), :] = totals[gone, :].astype(BF16)
                sent.append(halving(1))
                sent[1].start()
                yield
        size = height // data_size
        low = height - height // 4
        outgo[pl.ds(low, layers * size), :] = totals[: layers * size, :].astype(BF16)
        layer = data // 4
        for k in range(1, layers):
            to = lax.rem(layer + k, layers)
            src = outgo.at[pl.ds(pl.multiple_of(low + to * size, size), size)]
            dst = income.at[pl.ds(low + (k - 1) * size, size)]
            copy = remote(
                src, dst, red_send.at[which, 1 + k], red_recv.at[which, 1 + k],
                (to * 4 + lax.rem(data, 4), place),
            )
            copy.start()
            sent.append(copy)
        yield
        held = totals[pl.ds(pl.multiple_of(layer * size, size), size), :]
        for k in range(1, layers):
            sent[1 + k].wait_recv()
            held = held + income[pl.ds(low + (k - 1) * size, size), :].astype(F32)
        region = offset
        offset = offset + layer * size
        sum_ref[pl.ds(pl.multiple_of(offset, size), size), columns] = held.astype(BF16)

        count = [0]

        def spread(start, size, where):
            rows = sum_ref.at[pl.ds(pl.multiple_of(start, 16), size), columns]
            n = count[0]
            count[0] += 1
            copy = remote(rows, rows, all_send.at[which, n], all_recv.at[which, n], where)
            copy.start()
            sent.append(copy)
            return copy

        copies = [
            spread(offset, size, (lax.rem(layer + k, layers) * 4 + lax.rem(data, 4), place))
            for k in range(1, layers)
        ]
        yield
        for copy in copies:
            copy.wait_recv()
        offset = region
        size = layers * size
        mirror = (1 - 2 * place) * height
        if last == "x":
            copy = spread(offset, size, toward(1))
            yield
            copy.wait_recv()
            offset = offset - bit(1) * size
            size = 2 * size
            first = spread(offset, size, across_x)
            near = spread(offset, size, toward(0))
            yield
            first.wait_recv()
            back = spread(offset + mirror, size, toward(0))
            yield
            near.wait_recv()
            back.wait_recv()
        else:
            first = spread(offset, size, across_x)
            second = spread(offset, size, toward(1))
            yield
            first.wait_recv()
            third = spread(offset + mirror, size, toward(1))
            yield
            second.wait_recv()
            offset = offset - bit(1) * size
            size = 2 * size
            near = spread(offset, size, toward(0))
            third.wait_recv()
            back = spread(offset + mirror, size, toward(0))
            yield
            near.wait_recv()
            back.wait_recv()
        for copy in sent:
            copy.wait_send()

    part_a[:, :width] = dot_first(gated[:, mine], og[...]).astype(BF16)
    ev_mine = ev[:, mine]
    part_a[:, width:] = dot_first(ev_mine, gp[:, :width]).astype(BF16)
    run_a = travel(0, part_a, income_a, outgo_a, totals_a, 0, "x")
    next(run_a)

    pairs = width // 128
    piece = width // 2

    def late(part, which):
        for n in range(3):
            cols = slice((n + 1) * width + which * piece, (n + 1) * width + (which + 1) * piece)
            part[:, n * piece : (n + 1) * piece] = dot_first(ev_mine, gp[:, cols]).astype(BF16)

    pl.loop(0, pairs // 2)(back_pair)
    next(run_a)
    late(part_b, 0)
    run_b = travel(1, part_b, income_b, outgo_b, totals_b, 2 * width, "y")
    next(run_b)
    pl.loop(pairs // 2, pairs)(back_pair)
    next(run_a)
    next(run_b)
    late(part_c, 1)
    run_c = travel(2, part_c, income_c, outgo_c, totals_c, 2 * width + 3 * piece, "y")
    next(run_c)
    next(run_a)
    next(run_b)

    grad_events = (og[...].astype(F32) + dot_rows(gp[...], weight_ref[...])).astype(BF16)
    pack[...] = jnp.dot(chosen_slots[...], grad_events, preferred_element_type=F32).astype(BF16)
    here = pl.ds(pl.multiple_of(data * block, block), block)
    local = pltpu.make_async_copy(pack.at[here], got_ref.at[here], local_sem)
    local.start()

    fourth = data_size // 4
    turns = [[k for k in (g + fourth, g + 2 * fourth, g + 3 * fourth, g) if k] for g in range(fourth)]
    running = [run_a, run_b, run_c]
    for count in (1, 1, 1, 1, 0, 0):
        for _ in range(count):
            for k in turns.pop(0):
                row_copy(k).start()
        running = [run for run in running if next(run, "end") != "end"]

    local.wait()

    @pl.loop(1, data_size)
    def _(k):
        row_copy(k).wait_recv()
        mark_copy(k).wait_recv()

    sender = lax.broadcasted_iota(jnp.int32, (data_size, data_size * MARK), 0)
    flat = lax.broadcasted_iota(jnp.int32, (data_size, data_size * MARK), 1)
    found = []
    for n in range(2):
        pick = (flat == sender * MARK + n).astype(BF16)
        found.append(jnp.dot(pick, marks_in[...], preferred_element_type=F32).astype(BF16))

    def keys_of(count, per, lane_of):
        row = lax.broadcasted_iota(jnp.int32, (count, data_size), 0) // per
        of = (row == lax.broadcasted_iota(jnp.int32, (count, data_size), 1)).astype(BF16)
        high = jnp.dot(of, found[0], preferred_element_type=F32)
        low = jnp.dot(of, found[1], preferred_element_type=F32)
        spot_row = lane_of(lax.broadcasted_iota(jnp.int32, (count, 128), 0) % per)
        spot_lane = lax.broadcasted_iota(jnp.int32, (count, 128), 1)
        key = jnp.where(spot_row == spot_lane, high * 256.0 + low, 0.0)
        return jnp.sum(key, axis=1, keepdims=True)

    column = jnp.broadcast_to(keys_of(slots, block, lambda at: at), (slots, 128))
    line = jnp.transpose(column)[0:1, :]
    spot_line = lax.broadcasted_iota(jnp.int32, (1, slots), 1) % (2 * capacity)
    for t, out in enumerate((quotient_ref, remainder_ref)):
        wanted = keys_of(
            out.shape[0],
            2 * capacity,
            lambda at: at + t * capacity + jnp.where(at >= capacity, capacity, 0),
        )
        inside = (spot_line >= t * capacity) & (spot_line < (t + 1) * capacity) & (line > 0.0)
        match = ((wanted == line) & inside).astype(BF16)
        out[...] = jnp.dot(match, got_ref[...], preferred_element_type=F32)

    while running:
        running = [run for run in running if next(run, "end") != "end"]

    ev_copy.wait_send()
    og_copy.wait_send()

    info_copy.wait_send()

    @pl.loop(1, data_size)
    def _(k):
        row_copy(k).wait_send()
        mark_copy(k).wait_send()


def pair_body(
    events, out_grad, proj_weight, out_weight, lengths, tile_mask,
    quotient_shard, quotient_row, remainder_shard, remainder_row,
):
    half, width = events.shape
    data_size = lax.axis_size("dp")
    devices = 2 * data_size
    capacity = 3 * half // (2 * devices)
    full = 2 * half
    named = [quotient_shard, remainder_shard, quotient_row, remainder_row]
    info = jnp.stack(named + named)
    vmem = pl.BlockSpec(memory_space=pltpu.VMEM)
    smem = pl.BlockSpec(memory_space=pltpu.SMEM)
    layers = data_size // 4
    wides = (2 * width, 3 * width // 2, 3 * width // 2)
    quotient, remainder, sums = pl.pallas_call(
        lambda *refs: layer_kernel(data_size, *refs),
        name="layer",
        out_shape=(
            jax.ShapeDtypeStruct((devices * capacity, width), F32),
            jax.ShapeDtypeStruct((devices * capacity, width), F32),
            jax.ShapeDtypeStruct((full, 5 * width), BF16),
        ),
        in_specs=[smem] * 2 + [vmem] * 5,
        out_specs=(vmem, vmem, vmem),
        scratch_shapes=[
            pltpu.VMEM((full, width), BF16),
            pltpu.VMEM((full, width), BF16),
            pltpu.VMEM((full, 4 * width), BF16),
            pltpu.VMEM((full, 4 * width), F32),
            pltpu.VMEM((HEADS, full, full), BF16),
            pltpu.VMEM((HEADS, full, full), F32),
            pltpu.VMEM((full, width), F32),
            pltpu.VMEM((full, width), BF16),
            pltpu.VMEM((full, full), F32),
            pltpu.VMEM((full, 4 * width), BF16),
            pltpu.VMEM((full, width), BF16),
            pltpu.VMEM((data_size * 4 * capacity, width), BF16),
            pltpu.VMEM((data_size * 4 * capacity, width), BF16),
            pltpu.VMEM((16, half), jnp.int32),
            pltpu.VMEM((data_size * 4 * capacity, full), BF16),
            pltpu.VMEM((data_size * MARK, 128), BF16),
            pltpu.VMEM((data_size * MARK, 128), BF16),
            *[pltpu.VMEM((half, wide), BF16) for wide in wides],
            *[pltpu.VMEM((half, wide), BF16) for wide in wides],
            *[pltpu.VMEM((half, wide), BF16) for wide in wides],
            *[pltpu.VMEM((half // 2, wide), F32) for wide in wides],
            pltpu.SemaphoreType.DMA,
            pltpu.SemaphoreType.DMA((3,)),
            pltpu.SemaphoreType.DMA((3,)),
            pltpu.SemaphoreType.DMA((data_size,)),
            pltpu.SemaphoreType.DMA((data_size,)),
            pltpu.SemaphoreType.DMA((data_size,)),
            pltpu.SemaphoreType.DMA((data_size,)),
            pltpu.SemaphoreType.DMA((3, layers + 1)),
            pltpu.SemaphoreType.DMA((3, layers + 1)),
            pltpu.SemaphoreType.DMA((3, layers + 4)),
            pltpu.SemaphoreType.DMA((3, layers + 4)),
        ],
        compiler_params=pltpu.CompilerParams(
            collective_id=0, has_side_effects=True, vmem_limit_bytes=56 * 2**20
        ),
        cost_estimate=pl.CostEstimate(
            flops=10 * 10**9, bytes_accessed=8 * 2**20, transcendentals=4 * 10**6
        ),
    )(
        lengths, tile_mask, events, out_grad, proj_weight, out_weight, info,
    )
    piece = width // 2
    proj_grad = [sums[:, 2 * piece : 4 * piece]]
    for n in range(3):
        for h in range(2):
            start = (4 + 3 * h + n) * piece
            proj_grad.append(sums[:, start : start + piece])
    return (
        quotient,
        remainder,
        jnp.concatenate(proj_grad, axis=1).astype(F32),
        sums[:, :width].astype(F32),
    )


def pair_fits(mesh):
    data_size, loop_size = mesh.shape["dp"], mesh.shape["ctx"]
    return loop_size == 2 and data_size == 16


def solution(mesh):
    chosen = pair_body if pair_fits(mesh) else body
    in_specs = (
        P(("dp", "ctx"), None),
        P(("dp", "ctx"), None),
        P(),
        P(),
        P("dp", None),
        P("dp", None),
        P(("dp", "ctx")),
        P(("dp", "ctx")),
        P(("dp", "ctx")),
        P(("dp", "ctx")),
    )
    out_specs = (P(("dp", "ctx"), None), P(("dp", "ctx"), None), P(), P())
    return jax.shard_map(chosen, mesh=mesh, in_specs=in_specs, out_specs=out_specs, check_vma=False)
```
